128 devices in a mesh: ctx: 32 (over z, x, core), head: 4 (over y).
Axes of the slice: x: 4, y: 4, z: 4, core: 2. Of those that a mesh axis runs over, the one named last changes fastest.
Arguments:
- queries: bfloat16 [8192, 4096], P('ctx', 'head'), may hold values from -6 to 6
- key_rows: bfloat16 [8192, 4096], P('ctx', 'head'), may hold values from -6 to 6
- value_rows: bfloat16 [8192, 4096], P('ctx', 'head'), may hold values from -6 to 6
- norm_gain: float32 [4096], P('head'), may hold values from 0.25 to 1.75
- out_weight: bfloat16 [4096, 6144], P('head'), may hold values from -0.09375 to 0.09375
- out_cotangent: bfloat16 [8192, 6144], P(('ctx', 'head')), may hold values from -6 to 6
Outputs:
- layer_out: bfloat16 [8192, 6144], P(('ctx', 'head'))
- query_grad: bfloat16 [8192, 4096], P('ctx', 'head')
- key_grad: bfloat16 [8192, 4096], P('ctx', 'head')
- value_grad: bfloat16 [8192, 4096], P('ctx', 'head')
The draws below stay inside these ranges and needn't reach their ends.
All inputs are finite; a program needn't handle non-finite values.
Results may differ from the reference program's by a relative error of at most 0.0065.
Values may be sent and summed in bfloat16 or wider, within the bound.
A program may use at most 128 MiB of HBM per device.

```python
import jax
import jax.numpy as jnp
from jax import lax

D = 6144
DH = 128
H = 32
TOK_DEV = 256
TOKENS = 8192
N_CTX = 32


def block_scale(own_key, dims, cuts, smallest, high):
    loudness = 1.0
    for position, shards_of in cuts:
        steps = jax.random.uniform(jax.random.fold_in(jax.random.fold_in(own_key, 6), position), (shards_of,), jnp.float32, smallest / len(cuts), high / len(cuts))
        loudness = loudness * jnp.repeat(jnp.exp(steps), dims[position] // shards_of).reshape((-1,) + (1,) * (len(dims) - 1 - position))
    return loudness


def bell_draw(rng, extent, width, bound, pieces=(), kind=jnp.bfloat16):
    array = width * jax.random.normal(rng, extent, jnp.float32)
    if pieces:
        array = array * block_scale(rng, extent, pieces, -0.22, 0.18)
    return jnp.clip(array, -bound, bound).astype(kind)


def setup_inputs(seed: int = 0) -> dict:
    keys = jax.random.split(jax.random.key(seed), 7)
    return {
        "queries": bell_draw(keys[0], (TOKENS, H * DH), 1.0, 6.0, ((0, 32), (1, 4))),
        "key_rows": bell_draw(keys[1], (TOKENS, H * DH), 1.0, 6.0, ((0, 32), (1, 4))),
        "value_rows": bell_draw(keys[2], (TOKENS, H * DH), 1.0, 6.0, ((0, 32), (1, 4))),
        "norm_gain": jnp.clip(1.0 + 0.15 * jax.random.normal(keys[3], (H * DH,), jnp.float32), 0.25, 1.75),
        "out_weight": bell_draw(keys[4], (H * DH, D), (H * DH) ** -0.5, 0.09375, ((0, 4),)),
        "out_cotangent": bell_draw(keys[5], (TOKENS, D), 1.0, 6.0, ((0, 128),)),
    }


def rounded(values):
    return lax.optimization_barrier(values.astype(jnp.bfloat16)).astype(jnp.float32)

def normalize(hidden, gain):
    scale = lax.rsqrt(lax.optimization_barrier(jnp.mean(hidden * hidden, axis=-1, keepdims=True)) + 1e-06)
    return hidden * scale * gain

def reference(queries, key_rows, value_rows, norm_gain, out_weight, out_cotangent):
    shape = (N_CTX, TOK_DEV, H, DH)
    query_blocks = queries.reshape(shape).astype(jnp.float32)
    key_blocks = key_rows.reshape(shape).astype(jnp.float32)
    value_blocks = value_rows.reshape(shape).astype(jnp.float32)
    causal = jnp.arange(TOK_DEV)[:, None] >= jnp.arange(TOK_DEV)[None, :]
    block_state = rounded(jnp.einsum('cthd,cthe->chde', key_blocks, value_blocks))
    zero_state = jnp.zeros_like(block_state[:1])
    prefix_state = rounded(jnp.concatenate([zero_state, jnp.cumsum(block_state, axis=0)[:-1]], axis=0))
    scores = jnp.einsum('cthd,cshd->chts', query_blocks, key_blocks)
    inner = rounded(jnp.where(causal, scores, 0.0))
    attn = jnp.einsum('chts,cshe->cthe', inner, value_blocks) + jnp.einsum('cthd,chde->cthe', query_blocks, prefix_state)
    gain = norm_gain.reshape(H, DH)
    normed = normalize(attn, gain).astype(jnp.bfloat16).reshape(TOKENS, H * DH)
    layer_out = jnp.dot(normed, out_weight, preferred_element_type=jnp.float32).astype(jnp.bfloat16)
    normed_grad = jnp.dot(out_cotangent, out_weight.T, preferred_element_type=jnp.float32).reshape(shape)
    unused, pullback = jax.vjp(lambda hidden: normalize(hidden, gain), attn)
    attn_grad = rounded(pullback(normed_grad)[0])
    grad_state = rounded(jnp.einsum('cthd,cthe->chde', query_blocks, attn_grad))
    flipped = jnp.cumsum(grad_state[::-1], axis=0)[::-1]
    suffix_state = rounded(jnp.concatenate([flipped[1:], zero_state], axis=0))
    inner_grad = rounded(jnp.where(causal, jnp.einsum('cthe,cshe->chts', attn_grad, value_blocks), 0.0))
    query_grad = jnp.einsum('chts,cshd->cthd', inner_grad, key_blocks) + jnp.einsum('cthe,chde->cthd', attn_grad, prefix_state)
    key_grad = jnp.einsum('chts,cthd->cshd', inner_grad, query_blocks) + jnp.einsum('cthe,chde->cthd', value_blocks, suffix_state)
    value_grad = jnp.einsum('chts,cthe->cshe', inner, attn_grad) + jnp.einsum('cthd,chde->cthe', key_blocks, suffix_state)
    flat = (TOKENS, H * DH)
    return (layer_out, query_grad.reshape(flat).astype(jnp.bfloat16), key_grad.reshape(flat).astype(jnp.bfloat16), value_grad.reshape(flat).astype(jnp.bfloat16))
```

```python
import functools

import jax
import jax.numpy as jnp
from jax import lax
from jax.experimental import pallas as pl
from jax.experimental.pallas import tpu as pltpu
from jax.sharding import PartitionSpec as P

DH = 128
MESH = pl.DeviceIdType.MESH
f32 = jnp.float32
bf16 = jnp.bfloat16


def nn(a, b):
    return jnp.dot(a, b, preferred_element_type=f32)


def nt(a, b):
    return lax.dot_general(a, b, (((1,), (1,)), ((), ())), preferred_element_type=f32)


def tn(a, b):
    return lax.dot_general(a, b, (((0,), (0,)), ((), ())), preferred_element_type=f32)


def kernel(
    n_ctx,
    n_head,
    chunk,
    q_hbm,
    k_hbm,
    v_hbm,
    gain,
    w_hbm,
    cot_hbm,
    lo_hbm,
    dq_hbm,
    dk_hbm,
    dv_hbm,
    q,
    k,
    v,
    w,
    cot,
    inner,
    attn,
    scale,
    normed,
    part,
    own,
    p,
    rel,
    fin_dn,
    fin_up,
    ng,
    ag,
    dq,
    dk,
    dv,
    dkb,
    dvb,
    lo,
    st_own,
    st_got,
    st_sum,
    st_pre,
    gs_own,
    gs_got,
    gs_sum,
    gs_suf,
    ld_sem,
    out_sem,
    ag_send,
    ag_recv,
    sc_send,
    sc_recv,
    rel_send,
    rel_recv,
    one_send,
    one_recv,
    two_send,
    two_recv,
):
    c = lax.axis_index("ctx")
    y = lax.axis_index("head")
    up = lax.rem(y + 1, n_head)
    down = lax.rem(y + n_head - 1, n_head)
    far = lax.rem(y + 2, n_head)
    tok, feat = q.shape
    heads = feat // DH
    rows = cot.shape[1]
    width = cot.shape[2]
    n_chunk = width // chunk
    half = rows // 2
    share = st_own.shape[0] // n_ctx

    loads = [
        pltpu.make_async_copy(src, dst, ld_sem.at[i])
        for i, (src, dst) in enumerate(
            ((k_hbm, k), (v_hbm, v), (q_hbm, q), (cot_hbm, cot.at[y]), (w_hbm, w))
        )
    ]
    for load in loads:
        load.start()

    barrier = pltpu.get_barrier_semaphore()

    def greet(i, carry):
        pl.semaphore_signal(
            barrier, inc=1, device_id=(lax.rem(c + i, n_ctx), y), device_id_type=MESH
        )
        return carry

    for near in (up, down):
        pl.semaphore_signal(barrier, inc=1, device_id=(c, near), device_id_type=MESH)
    lax.fori_loop(1, n_ctx, greet, 0)
    pl.semaphore_wait(barrier, n_ctx + 1)

    first, second = pl.ds(0, half), pl.ds(half, half)

    def hop(src, owner, piece, to, i):
        return pltpu.make_async_remote_copy(
            src_ref=src,
            dst_ref=cot.at[owner, piece],
            send_sem=ag_send.at[i],
            recv_sem=ag_recv.at[i],
            device_id=(c, to),
            device_id_type=MESH,
        )

    hops = [
        hop(cot_hbm.at[first], y, first, up, 0),
        hop(cot_hbm.at[second], y, second, down, 3),
        hop(cot_hbm.at[second], y, second, up, 1),
        hop(cot_hbm.at[first], y, first, down, 4),
    ]
    for h in hops:
        h.start()

    def lanes(h):
        return pl.ds(pl.multiple_of(h * DH, DH), DH)

    def piece_of(i):
        return pl.ds(pl.multiple_of(i * share, share), share)

    def exchange(src, dst, i):
        def step(j, carry):
            peer = lax.rem(c + j, n_ctx)
            pltpu.make_async_remote_copy(
                src_ref=src.at[piece_of(peer)],
                dst_ref=dst.at[piece_of(c)],
                send_sem=sc_send.at[i],
                recv_sem=sc_recv.at[i],
                device_id=(peer, y),
                device_id_type=MESH,
            ).start()
            return carry

        lax.fori_loop(1, n_ctx, step, 0)
        dst[piece_of(c), :] = src[piece_of(c), :]

    def exchanged(src, dst, i):
        whole = pl.ds(0, (n_ctx - 1) * share)
        all_of = pltpu.make_async_remote_copy(
            src_ref=src.at[whole],
            dst_ref=dst.at[whole],
            send_sem=sc_send.at[i],
            recv_sem=sc_recv.at[i],
            device_id=(lax.rem(c + 1, n_ctx), y),
            device_id_type=MESH,
        )
        all_of.wait_send()
        all_of.wait_recv()

    loads[0].wait()
    loads[1].wait()

    def state_step(h, carry):
        hs = lanes(h)
        st_own[hs, :] = tn(k[:, hs], v[:, hs]).astype(bf16)
        return carry

    lax.fori_loop(0, heads, state_step, 0)
    exchange(st_own, st_got, 0)

    loads[2].wait()
    causal = lax.broadcasted_iota(jnp.int32, (tok, tok), 0) >= lax.broadcasted_iota(
        jnp.int32, (tok, tok), 1
    )

    def inner_step(h, carry):
        hs = lanes(h)
        masked = jnp.where(causal, nt(q[:, hs], k[:, hs]), 0.0).astype(bf16)
        inner[h] = masked
        attn[:, hs] = nn(masked, v[:, hs])
        return carry

    lax.fori_loop(0, heads, inner_step, 0)

    exchanged(st_own, st_got, 0)

    def prefix_step(i, total):
        st_sum[piece_of(i), :] = total.astype(bf16)
        return total + st_got[piece_of(i), :].astype(f32)

    lax.fori_loop(0, n_ctx, prefix_step, jnp.zeros((share, DH), f32))
    exchange(st_sum, st_pre, 1)
    exchanged(st_sum, st_pre, 1)

    def norm_step(h, carry):
        hs = lanes(h)
        a = attn[:, hs] + nn(q[:, hs], st_pre[hs, :])
        r = lax.rsqrt(jnp.mean(a * a, axis=-1, keepdims=True) + 1e-06)
        x = a * r
        attn[:, hs] = x
        scale[h] = jnp.broadcast_to(r, x.shape)
        normed[:, hs] = (x * gain[:, hs]).astype(bf16)
        return carry

    lax.fori_loop(0, heads, norm_step, 0)

    hops[0].wait_recv()
    onward_up = hop(cot.at[down, first], down, first, up, 2)
    onward_up.start()
    hops[1].wait_recv()
    onward_down = hop(cot.at[up, second], up, second, down, 5)
    onward_down.start()

    loads[4].wait()

    def slab(owner):
        return pl.ds(pl.multiple_of(owner * rows, rows), rows)

    def columns(j):
        return pl.ds(pl.multiple_of(j * chunk, chunk), chunk)

    def relay(j, to):
        return pltpu.make_async_remote_copy(
            src_ref=p.at[slab(far), columns(j)],
            dst_ref=rel.at[:, columns(j)],
            send_sem=rel_send.at[j],
            recv_sem=rel_recv.at[j],
            device_id=(c, to),
            device_id_type=MESH,
        )

    def single(j, to, dst):
        return pltpu.make_async_remote_copy(
            src_ref=p.at[slab(to), columns(j)],
            dst_ref=dst.at[:, columns(j)],
            send_sem=one_send.at[j],
            recv_sem=one_recv.at[j],
            device_id=(c, to),
            device_id_type=MESH,
        )

    def double(j, to, dst):
        return pltpu.make_async_remote_copy(
            src_ref=rel.at[:, columns(j)],
            dst_ref=dst.at[:, columns(j)],
            send_sem=two_send.at[j],
            recv_sem=two_recv.at[j],
            device_id=(c, to),
            device_id_type=MESH,
        )

    n_half = n_chunk // 2

    def project(j):
        cs = columns(j)
        product = nn(normed[...], w[:, cs])
        part[...] = product
        p[:, cs] = product.astype(bf16)
        own[:, cs] = part[slab(y), :]

    def project_step(i, carry):
        j = i
        project(j)
        relay(j, up).start()
        single(j, down, fin_up).start()
        j = i + n_half
        project(j)
        relay(j, down).start()
        single(j, up, fin_dn).start()
        return carry

    lax.fori_loop(0, n_half, project_step, 0)

    loads[3].wait()
    hops[2].wait_recv()
    hops[3].wait_recv()
    onward_up.wait_recv()
    onward_down.wait_recv()

    wide = 2 * DH

    def ng_step(i, carry):
        rs = pl.ds(pl.multiple_of(i * wide, wide), wide)
        ng[:, rs] = nt(cot[...].reshape(tok, width), w[rs, :])
        return carry

    lax.fori_loop(0, feat // wide, ng_step, 0)

    def norm_back_step(h, carry):
        hs = lanes(h)
        x = attn[:, hs]
        g = ng[:, hs] * gain[:, hs]
        a = scale[h] * (g - x * jnp.mean(g * x, axis=-1, keepdims=True))
        a = a.astype(bf16)
        ag[:, hs] = a
        gs_own[hs, :] = tn(q[:, hs], a).astype(bf16)
        return carry

    lax.fori_loop(0, heads, norm_back_step, 0)
    exchange(gs_own, gs_got, 2)

    def grad_step(h, carry):
        hs = lanes(h)
        a = ag[:, hs]
        masked = jnp.where(causal, nt(a, v[:, hs]), 0.0).astype(bf16)
        dq[:, hs] = (nn(masked, k[:, hs]) + nt(a, st_pre[hs, :])).astype(bf16)
        dk[:, hs] = tn(masked, q[:, hs])
        dv[:, hs] = tn(inner[h], a)
        return carry

    lax.fori_loop(0, heads, grad_step, 0)
    out_dq = pltpu.make_async_copy(dq, dq_hbm, out_sem.at[0])
    out_dq.start()

    exchanged(gs_own, gs_got, 2)

    def suffix_step(i, total):
        at = piece_of(n_ctx - 1 - i)
        gs_sum[at, :] = total.astype(bf16)
        return total + gs_got[at, :].astype(f32)

    lax.fori_loop(0, n_ctx, suffix_step, jnp.zeros((share, DH), f32))
    exchange(gs_sum, gs_suf, 3)

    def relay_step(i, carry):
        for j, src, to, dst in ((i, down, up, fin_dn), (i + n_half, up, down, fin_up)):
            cs = columns(j)
            relay(j, to).wait_recv()
            rel[:, cs] = (rel[:, cs].astype(f32) + p[slab(to), cs].astype(f32)).astype(bf16)
            double(j, to, dst).start()
        return carry

    lax.fori_loop(0, n_half, relay_step, 0)

    exchanged(gs_sum, gs_suf, 3)

    def last_step(h, carry):
        hs = lanes(h)
        dkb[:, hs] = (dk[:, hs] + nt(v[:, hs], gs_suf[hs, :])).astype(bf16)
        dvb[:, hs] = (dv[:, hs] + nn(k[:, hs], gs_suf[hs, :])).astype(bf16)
        return carry

    lax.fori_loop(0, heads, last_step, 0)
    out_dk = pltpu.make_async_copy(dkb, dk_hbm, out_sem.at[1])
    out_dv = pltpu.make_async_copy(dvb, dv_hbm, out_sem.at[2])
    out_dk.start()
    out_dv.start()

    def sum_step(i, carry):
        for j, to, one, two in ((i, down, fin_up, fin_dn), (i + n_half, up, fin_dn, fin_up)):
            cs = columns(j)
            single(j, to, one).wait_recv()
            double(j, to, two).wait_recv()
            lo[:, cs] = (
                own[:, cs] + (fin_dn[:, cs].astype(f32) + fin_up[:, cs].astype(f32))
            ).astype(bf16)
        return carry

    lax.fori_loop(0, n_half, sum_step, 0)
    out_lo = pltpu.make_async_copy(lo, lo_hbm, out_sem.at[3])
    out_lo.start()

    for h in (*hops, onward_up, onward_down):
        h.wait_send()

    def sent_step(j, carry):
        relay(j, up).wait_send()
        single(j, up, fin_dn).wait_send()
        double(j, up, fin_dn).wait_send()
        return carry

    lax.fori_loop(0, n_chunk, sent_step, 0)
    for out in (out_dq, out_dk, out_dv, out_lo):
        out.wait()


def per_device(n_ctx, n_head, queries, key_rows, value_rows, norm_gain, out_weight, out_cotangent):
    tok, feat = queries.shape
    rows, width = out_cotangent.shape
    heads = feat // DH
    chunk = width // 6
    n_chunk = width // chunk
    state = pltpu.VMEM((feat, DH), bf16)
    any_space = pl.BlockSpec(memory_space=pl.ANY)
    vmem = pl.BlockSpec(memory_space=pltpu.VMEM)
    dma = pltpu.SemaphoreType.DMA
    return pl.pallas_call(
        functools.partial(kernel, n_ctx, n_head, chunk),
        out_shape=(
            jax.ShapeDtypeStruct((rows, width), bf16),
            jax.ShapeDtypeStruct((tok, feat), bf16),
            jax.ShapeDtypeStruct((tok, feat), bf16),
            jax.ShapeDtypeStruct((tok, feat), bf16),
        ),
        in_specs=[any_space, any_space, any_space, vmem, any_space, any_space],
        out_specs=(any_space, any_space, any_space, any_space),
        scratch_shapes=[
            pltpu.VMEM((tok, feat), bf16),
            pltpu.VMEM((tok, feat), bf16),
            pltpu.VMEM((tok, feat), bf16),
            pltpu.VMEM((feat, width), bf16),
            pltpu.VMEM((n_head, rows, width), bf16),
            pltpu.VMEM((heads, tok, tok), bf16),
            pltpu.VMEM((tok, feat), f32),
            pltpu.VMEM((heads, tok, DH), f32),
            pltpu.VMEM((tok, feat), bf16),
            pltpu.VMEM((tok, chunk), f32),
            pltpu.VMEM((rows, width), f32),
            pltpu.VMEM((tok, width), bf16),
            pltpu.VMEM((rows, width), bf16),
            pltpu.VMEM((rows, width), bf16),
            pltpu.VMEM((rows, width), bf16),
            pltpu.VMEM((tok, feat), f32),
            pltpu.VMEM((tok, feat), bf16),
            pltpu.VMEM((tok, feat), bf16),
            pltpu.VMEM((tok, feat), f32),
            pltpu.VMEM((tok, feat), f32),
            pltpu.VMEM((tok, feat), bf16),
            pltpu.VMEM((tok, feat), bf16),
            pltpu.VMEM((rows, width), bf16),
            *[state] * 8,
            dma((5,)),
            dma((4,)),
            dma((6,)),
            dma((6,)),
            dma((4,)),
            dma((4,)),
            *[dma((n_chunk,))] * 6,
        ],
        compiler_params=pltpu.CompilerParams(
            collective_id=0, has_side_effects=True, vmem_limit_bytes=56 * 1024 * 1024
        ),
        cost_estimate=pl.CostEstimate(
            flops=8_000_000_000, bytes_accessed=18_000_000, transcendentals=0
        ),
    )(
        queries,
        key_rows,
        value_rows,
        norm_gain.reshape(1, feat),
        out_weight,
        out_cotangent,
    )


def solution(mesh):
    in_specs = (
        P("ctx", "head"),
        P("ctx", "head"),
        P("ctx", "head"),
        P("head"),
        P("head", None),
        P(("ctx", "head"), None),
    )
    out_specs = (P(("ctx", "head"), None), P("ctx", "head"), P("ctx", "head"), P("ctx", "head"))
    return jax.shard_map(
        functools.partial(per_device, mesh.shape["ctx"], mesh.shape["head"]),
        mesh=mesh,
        in_specs=in_specs,
        out_specs=out_specs,
        check_vma=False,
    )
```

```python
import functools

import jax
import jax.numpy as jnp
from jax import lax
from jax.experimental import pallas as pl
from jax.experimental.pallas import tpu as pltpu
from jax.sharding import PartitionSpec as P

DH = 128
MESH = pl.DeviceIdType.MESH
f32 = jnp.float32
bf16 = jnp.bfloat16


def nn(a, b):
    return jnp.dot(a, b, preferred_element_type=f32)


def nt(a, b):
    return lax.dot_general(a, b, (((1,), (1,)), ((), ())), preferred_element_type=f32)


def tn(a, b):
    return lax.dot_general(a, b, (((0,), (0,)), ((), ())), preferred_element_type=f32)


def kernel(
    n_ctx,
    n_head,
    chunk,
    q_hbm,
    k_hbm,
    v_hbm,
    gain,
    w_hbm,
    cot_hbm,
    lo,
    dq,
    dkb,
    dvb,
    q,
    k,
    v,
    w,
    cot,
    inner,
    attn,
    scale,
    normed,
    part,
    own,
    p,
    rel,
    fin_dn,
    fin_up,
    ng,
    ag,
    dk,
    dv,
    st_own,
    st_got,
    st_sum,
    st_pre,
    gs_own,
    gs_got,
    gs_sum,
    gs_suf,
    ld_sem,
    ag_send,
    ag_recv,
    sc_send,
    sc_recv,
    rel_send,
    rel_recv,
    one_send,
    one_recv,
    two_send,
    two_recv,
):
    c = lax.axis_index("ctx")
    y = lax.axis_index("head")
    up = lax.rem(y + 1, n_head)
    down = lax.rem(y + n_head - 1, n_head)
    far = lax.rem(y + 2, n_head)
    tok, feat = q.shape
    heads = feat // DH
    rows = cot.shape[1]
    width = cot.shape[2]
    n_chunk = width // chunk
    half = rows // 2
    share = st_own.shape[0] // n_ctx

    loads = [
        pltpu.make_async_copy(src, dst, ld_sem.at[i])
        for i, (src, dst) in enumerate(
            ((k_hbm, k), (v_hbm, v), (q_hbm, q), (cot_hbm, cot.at[y]), (w_hbm, w))
        )
    ]
    for load in loads:
        load.start()

    barrier = pltpu.get_barrier_semaphore()

    def greet(i, carry):
        pl.semaphore_signal(
            barrier, inc=1, device_id=(lax.rem(c + i, n_ctx), y), device_id_type=MESH
        )
        return carry

    for near in (up, down):
        pl.semaphore_signal(barrier, inc=1, device_id=(c, near), device_id_type=MESH)
    lax.fori_loop(1, n_ctx, greet, 0)
    pl.semaphore_wait(barrier, n_ctx + 1)

    first, second = pl.ds(0, half), pl.ds(half, half)

    def hop(src, owner, piece, to, i):
        return pltpu.make_async_remote_copy(
            src_ref=src,
            dst_ref=cot.at[owner, piece],
            send_sem=ag_send.at[i],
            recv_sem=ag_recv.at[i],
            device_id=(c, to),
            device_id_type=MESH,
        )

    hops = [
        hop(cot_hbm.at[first], y, first, up, 0),
        hop(cot_hbm.at[second], y, second, down, 3),
        hop(cot_hbm.at[second], y, second, up, 1),
        hop(cot_hbm.at[first], y, first, down, 4),
    ]
    for h in hops:
        h.start()

    def lanes(h):
        return pl.ds(pl.multiple_of(h * DH, DH), DH)

    def piece_of(i):
        return pl.ds(pl.multiple_of(i * share, share), share)

    def exchange(src, dst, i):
        def step(j, carry):
            peer = lax.rem(c + j, n_ctx)
            pltpu.make_async_remote_copy(
                src_ref=src.at[piece_of(peer)],
                dst_ref=dst.at[piece_of(c)],
                send_sem=sc_send.at[i],
                recv_sem=sc_recv.at[i],
                device_id=(peer, y),
                device_id_type=MESH,
            ).start()
            return carry

        lax.fori_loop(1, n_ctx, step, 0)
        dst[piece_of(c), :] = src[piece_of(c), :]

    def exchanged(src, dst, i):
        whole = pl.ds(0, (n_ctx - 1) * share)
        all_of = pltpu.make_async_remote_copy(
            src_ref=src.at[whole],
            dst_ref=dst.at[whole],
            send_sem=sc_send.at[i],
            recv_sem=sc_recv.at[i],
            device_id=(lax.rem(c + 1, n_ctx), y),
            device_id_type=MESH,
        )
        all_of.wait_send()
        all_of.wait_recv()

    loads[0].wait()
    loads[1].wait()

    def state_step(h, carry):
        hs = lanes(h)
        st_own[hs, :] = tn(k[:, hs], v[:, hs]).astype(bf16)
        return carry

    lax.fori_loop(0, heads, state_step, 0)
    exchange(st_own, st_got, 0)

    loads[2].wait()
    causal = lax.broadcasted_iota(jnp.int32, (tok, tok), 0) >= lax.broadcasted_iota(
        jnp.int32, (tok, tok), 1
    )

    def inner_step(h, carry):
        hs = lanes(h)
        masked = jnp.where(causal, nt(q[:, hs], k[:, hs]), 0.0).astype(bf16)
        inner[h] = masked
        attn[:, hs] = nn(masked, v[:, hs])
        return carry

    lax.fori_loop(0, heads, inner_step, 0)

    exchanged(st_own, st_got, 0)

    def prefix_step(i, total):
        st_sum[piece_of(i), :] = total.astype(bf16)
        return total + st_got[piece_of(i), :].astype(f32)

    lax.fori_loop(0, n_ctx, prefix_step, jnp.zeros((share, DH), f32))
    exchange(st_sum, st_pre, 1)
    exchanged(st_sum, st_pre, 1)

    def norm_step(h, carry):
        hs = lanes(h)
        a = attn[:, hs] + nn(q[:, hs], st_pre[hs, :])
        r = lax.rsqrt(jnp.mean(a * a, axis=-1, keepdims=True) + 1e-06)
        x = a * r
        attn[:, hs] = x
        scale[h] = jnp.broadcast_to(r, x.shape)
        normed[:, hs] = (x * gain[:, hs]).astype(bf16)
        return carry

    lax.fori_loop(0, heads, norm_step, 0)

    hops[0].wait_recv()
    onward_up = hop(cot.at[down, first], down, first, up, 2)
    onward_up.start()
    hops[1].wait_recv()
    onward_down = hop(cot.at[up, second], up, second, down, 5)
    onward_down.start()

    loads[4].wait()

    def slab(owner):
        return pl.ds(pl.multiple_of(owner * rows, rows), rows)

    def columns(j):
        return pl.ds(pl.multiple_of(j * chunk, chunk), chunk)

    def relay(j, to):
        return pltpu.make_async_remote_copy(
            src_ref=p.at[slab(far), columns(j)],
            dst_ref=rel.at[:, columns(j)],
            send_sem=rel_send.at[j],
            recv_sem=rel_recv.at[j],
            device_id=(c, to),
            device_id_type=MESH,
        )

    def single(j, to, dst):
        return pltpu.make_async_remote_copy(
            src_ref=p.at[slab(to), columns(j)],
            dst_ref=dst.at[:, columns(j)],
            send_sem=one_send.at[j],
            recv_sem=one_recv.at[j],
            device_id=(c, to),
            device_id_type=MESH,
        )

    def double(j, to, dst):
        return pltpu.make_async_remote_copy(
            src_ref=rel.at[:, columns(j)],
            dst_ref=dst.at[:, columns(j)],
            send_sem=two_send.at[j],
            recv_sem=two_recv.at[j],
            device_id=(c, to),
            device_id_type=MESH,
        )

    n_half = n_chunk // 2

    def project(j):
        cs = columns(j)
        product = nn(normed[...], w[:, cs])
        part[...] = product
        p[:, cs] = product.astype(bf16)
        own[:, cs] = part[slab(y), :]

    def project_step(i, carry):
        j = i
        project(j)
        relay(j, up).start()
        single(j, down, fin_up).start()
        j = i + n_half
        project(j)
        relay(j, down).start()
        single(j, up, fin_dn).start()
        return carry

    lax.fori_loop(0, n_half, project_step, 0)

    loads[3].wait()
    hops[2].wait_recv()
    hops[3].wait_recv()
    onward_up.wait_recv()
    onward_down.wait_recv()

    wide = 2 * DH

    def ng_step(i, carry):
        rs = pl.ds(pl.multiple_of(i * wide, wide), wide)
        ng[:, rs] = nt(cot[...].reshape(tok, width), w[rs, :])
        return carry

    lax.fori_loop(0, feat // wide, ng_step, 0)

    def norm_back_step(h, carry):
        hs = lanes(h)
        x = attn[:, hs]
        g = ng[:, hs] * gain[:, hs]
        a = scale[h] * (g - x * jnp.mean(g * x, axis=-1, keepdims=True))
        a = a.astype(bf16)
        ag[:, hs] = a
        gs_own[hs, :] = tn(q[:, hs], a).astype(bf16)
        return carry

    lax.fori_loop(0, heads, norm_back_step, 0)
    exchange(gs_own, gs_got, 2)

    def grad_step(h, carry):
        hs = lanes(h)
        a = ag[:, hs]
        masked = jnp.where(causal, nt(a, v[:, hs]), 0.0).astype(bf16)
        dq[:, hs] = (nn(masked, k[:, hs]) + nt(a, st_pre[hs, :])).astype(bf16)
        dk[:, hs] = tn(masked, q[:, hs])
        dv[:, hs] = tn(inner[h], a)
        return carry

    lax.fori_loop(0, heads, grad_step, 0)

    exchanged(gs_own, gs_got, 2)

    def suffix_step(i, total):
        at = piece_of(n_ctx - 1 - i)
        gs_sum[at, :] = total.astype(bf16)
        return total + gs_got[at, :].astype(f32)

    lax.fori_loop(0, n_ctx, suffix_step, jnp.zeros((share, DH), f32))
    exchange(gs_sum, gs_suf, 3)

    def relay_step(i, carry):
        for j, src, to, dst in ((i, down, up, fin_dn), (i + n_half, up, down, fin_up)):
            cs = columns(j)
            relay(j, to).wait_recv()
            rel[:, cs] = (rel[:, cs].astype(f32) + p[slab(to), cs].astype(f32)).astype(bf16)
            double(j, to, dst).start()
        return carry

    lax.fori_loop(0, n_half, relay_step, 0)

    exchanged(gs_sum, gs_suf, 3)

    def last_step(h, carry):
        hs = lanes(h)
        dkb[:, hs] = (dk[:, hs] + nt(v[:, hs], gs_suf[hs, :])).astype(bf16)
        dvb[:, hs] = (dv[:, hs] + nn(k[:, hs], gs_suf[hs, :])).astype(bf16)
        return carry

    lax.fori_loop(0, heads, last_step, 0)

    def sum_step(i, carry):
        for j, to, one, two in ((i, down, fin_up, fin_dn), (i + n_half, up, fin_dn, fin_up)):
            cs = columns(j)
            single(j, to, one).wait_recv()
            double(j, to, two).wait_recv()
            lo[:, cs] = (
                own[:, cs] + (fin_dn[:, cs].astype(f32) + fin_up[:, cs].astype(f32))
            ).astype(bf16)
        return carry

    lax.fori_loop(0, n_half, sum_step, 0)

    for h in (*hops, onward_up, onward_down):
        h.wait_send()

    def sent_step(j, carry):
        relay(j, up).wait_send()
        single(j, up, fin_dn).wait_send()
        double(j, up, fin_dn).wait_send()
        return carry

    lax.fori_loop(0, n_chunk, sent_step, 0)


def store_kernel(*refs):
    sources, results, sem = refs[:4], refs[4:8], refs[8]
    copies = [
        pltpu.make_async_copy(src, dst, sem.at[i])
        for i, (src, dst) in enumerate(zip(sources, results))
    ]
    for copy in copies:
        copy.start()
    for copy in copies:
        copy.wait()


def per_device(n_ctx, n_head, queries, key_rows, value_rows, norm_gain, out_weight, out_cotangent):
    tok, feat = queries.shape
    rows, width = out_cotangent.shape
    heads = feat // DH
    chunk = width // 6
    n_chunk = width // chunk
    state = pltpu.VMEM((feat, DH), bf16)
    any_space = pl.BlockSpec(memory_space=pl.ANY)
    vmem = pl.BlockSpec(memory_space=pltpu.VMEM)
    dma = pltpu.SemaphoreType.DMA
    results = pl.pallas_call(
        functools.partial(kernel, n_ctx, n_head, chunk),
        out_shape=(
            pltpu.VMEM((rows, width), bf16),
            pltpu.VMEM((tok, feat), bf16),
            pltpu.VMEM((tok, feat), bf16),
            pltpu.VMEM((tok, feat), bf16),
        ),
        in_specs=[any_space, any_space, any_space, vmem, any_space, any_space],
        out_specs=(vmem, vmem, vmem, vmem),
        scratch_shapes=[
            pltpu.VMEM((tok, feat), bf16),
            pltpu.VMEM((tok, feat), bf16),
            pltpu.VMEM((tok, feat), bf16),
            pltpu.VMEM((feat, width), bf16),
            pltpu.VMEM((n_head, rows, width), bf16),
            pltpu.VMEM((heads, tok, tok), bf16),
            pltpu.VMEM((tok, feat), f32),
            pltpu.VMEM((heads, tok, DH), f32),
            pltpu.VMEM((tok, feat), bf16),
            pltpu.VMEM((tok, chunk), f32),
            pltpu.VMEM((rows, width), f32),
            pltpu.VMEM((tok, width), bf16),
            pltpu.VMEM((rows, width), bf16),
            pltpu.VMEM((rows, width), bf16),
            pltpu.VMEM((rows, width), bf16),
            pltpu.VMEM((tok, feat), f32),
            pltpu.VMEM((tok, feat), bf16),
            pltpu.VMEM((tok, feat), f32),
            pltpu.VMEM((tok, feat), f32),
            *[state] * 8,
            dma((5,)),
            dma((6,)),
            dma((6,)),
            dma((4,)),
            dma((4,)),
            *[dma((n_chunk,))] * 6,
        ],
        compiler_params=pltpu.CompilerParams(
            collective_id=0, has_side_effects=True, vmem_limit_bytes=60 * 1024 * 1024
        ),
        cost_estimate=pl.CostEstimate(
            flops=8_000_000_000, bytes_accessed=18_000_000, transcendentals=0
        ),
    )(
        queries,
        key_rows,
        value_rows,
        norm_gain.reshape(1, feat),
        out_weight,
        out_cotangent,
    )
    return pl.pallas_call(
        store_kernel,
        out_shape=tuple(jax.ShapeDtypeStruct(r.shape, r.dtype) for r in results),
        in_specs=[vmem] * 4,
        out_specs=(any_space,) * 4,
        scratch_shapes=[dma((4,))],
        compiler_params=pltpu.CompilerParams(vmem_limit_bytes=1024 * 1024),
    )(*(pltpu.with_memory_space_constraint(r, pltpu.VMEM) for r in results))


def solution(mesh):
    in_specs = (
        P("ctx", "head"),
        P("ctx", "head"),
        P("ctx", "head"),
        P("head"),
        P("head", None),
        P(("ctx", "head"), None),
    )
    out_specs = (P(("ctx", "head"), None), P("ctx", "head"), P("ctx", "head"), P("ctx", "head"))
    return jax.shard_map(
        functools.partial(per_device, mesh.shape["ctx"], mesh.shape["head"]),
        mesh=mesh,
        in_specs=in_specs,
        out_specs=out_specs,
        check_vma=False,
    )
```

```python
import functools

import jax
import jax.numpy as jnp
from jax import lax
from jax.experimental import pallas as pl
from jax.experimental.pallas import tpu as pltpu
from jax.sharding import PartitionSpec as P

DH = 128
MESH = pl.DeviceIdType.MESH
f32 = jnp.float32
bf16 = jnp.bfloat16


def nn(a, b):
    return jnp.dot(a, b, preferred_element_type=f32)


def nt(a, b):
    return lax.dot_general(a, b, (((1,), (1,)), ((), ())), preferred_element_type=f32)


def tn(a, b):
    return lax.dot_general(a, b, (((0,), (0,)), ((), ())), preferred_element_type=f32)


def kernel(
    n_ctx,
    n_head,
    chunk,
    q_hbm,
    k_hbm,
    v_hbm,
    gain,
    w_hbm,
    cot_hbm,
    lo,
    dq,
    dkb,
    dvb,
    q,
    k,
    v,
    w,
    cot,
    inner,
    attn,
    scale,
    normed,
    part,
    own,
    p,
    rel,
    fin_dn,
    fin_up,
    ng,
    ag,
    dk,
    dv,
    st_own,
    st_got,
    st_sum,
    st_pre,
    gs_own,
    gs_got,
    gs_sum,
    gs_suf,
    ld_sem,
    ready,
    ag_send,
    ag_recv,
    sc_send,
    sc_recv,
    rel_send,
    rel_recv,
    one_send,
    one_recv,
    two_send,
    two_recv,
):
    c = lax.axis_index("ctx")
    y = lax.axis_index("head")
    up = lax.rem(y + 1, n_head)
    down = lax.rem(y + n_head - 1, n_head)
    far = lax.rem(y + 2, n_head)
    tok, feat = q.shape
    heads = feat // DH
    rows = cot.shape[1]
    width = cot.shape[2]
    n_chunk = width // chunk
    half = rows // 2
    wing = width // 2
    share = st_own.shape[0] // n_ctx

    loads = [
        pltpu.make_async_copy(src, dst, ld_sem.at[i])
        for i, (src, dst) in enumerate(
            ((k_hbm, k), (v_hbm, v), (q_hbm, q), (cot_hbm, cot.at[y]), (w_hbm, w))
        )
    ]
    for load in loads:
        load.start()

    barrier = pltpu.get_barrier_semaphore()

    def greet(i, carry):
        pl.semaphore_signal(barrier, inc=1, device_id=(i, y), device_id_type=MESH)
        return carry

    def answer(i, carry):
        pl.semaphore_signal(ready, inc=1, device_id=(i, y), device_id_type=MESH)
        return carry

    for near in (up, down):
        pl.semaphore_signal(barrier, inc=1, device_id=(c, near), device_id_type=MESH)
    lax.fori_loop(c + 1, n_ctx, greet, 0)
    pl.semaphore_wait(barrier, c + 2)

    def quarter(r, h):
        return pl.ds(r * half, half), pl.ds(h * wing, wing)

    def hop(src, owner, r, h, to, i):
        return pltpu.make_async_remote_copy(
            src_ref=src.at[quarter(r, h)],
            dst_ref=cot.at[(owner, *quarter(r, h))],
            send_sem=ag_send.at[i],
            recv_sem=ag_recv.at[i],
            device_id=(c, to),
            device_id_type=MESH,
        )

    ups = [hop(cot_hbm, y, r, h, up, 2 * h + r) for h in (0, 1) for r in (0, 1)]
    downs = [hop(cot_hbm, y, 1 - r, h, down, 4 + 2 * h + r) for h in (0, 1) for r in (0, 1)]
    for one, other in zip(ups, downs):
        one.start()
        other.start()
    lax.fori_loop(0, c, answer, 0)

    def onward(h):
        ups[2 * h].wait_recv()
        on_up = hop(cot.at[down], down, 0, h, up, 8 + h)
        on_up.start()
        downs[2 * h].wait_recv()
        on_down = hop(cot.at[up], up, 1, h, down, 10 + h)
        on_down.start()
        return on_up, on_down

    def lanes(h):
        return pl.ds(pl.multiple_of(h * DH, DH), DH)

    def piece_of(i):
        return pl.ds(pl.multiple_of(i * share, share), share)

    def exchange(src, dst, i):
        def step(j, carry):
            peer = lax.rem(c + 1 + lax.rem(j + n_ctx // 2, n_ctx - 1), n_ctx)
            pltpu.make_async_remote_copy(
                src_ref=src.at[piece_of(peer)],
                dst_ref=dst.at[piece_of(c)],
                send_sem=sc_send.at[i],
                recv_sem=sc_recv.at[i],
                device_id=(peer, y),
                device_id_type=MESH,
            ).start()
            return carry

        lax.fori_loop(1, n_ctx, step, 0)
        dst[piece_of(c), :] = src[piece_of(c), :]

    def exchanged(src, dst, i):
        whole = pl.ds(0, (n_ctx - 1) * share)
        all_of = pltpu.make_async_remote_copy(
            src_ref=src.at[whole],
            dst_ref=dst.at[whole],
            send_sem=sc_send.at[i],
            recv_sem=sc_recv.at[i],
            device_id=(lax.rem(c + 1, n_ctx), y),
            device_id_type=MESH,
        )
        all_of.wait_send()
        all_of.wait_recv()

    loads[0].wait()
    loads[1].wait()

    def state_step(h, carry):
        hs = lanes(h)
        st_own[hs, :] = tn(k[:, hs], v[:, hs]).astype(bf16)
        return carry

    lax.fori_loop(0, heads, state_step, 0)

    @pl.when(c < n_ctx - 1)
    def _():
        pl.semaphore_wait(ready, n_ctx - 1 - c)

    exchange(st_own, st_got, 0)

    loads[2].wait()
    causal = lax.broadcasted_iota(jnp.int32, (tok, tok), 0) >= lax.broadcasted_iota(
        jnp.int32, (tok, tok), 1
    )

    def inner_step(h, carry):
        hs = lanes(h)
        masked = jnp.where(causal, nt(q[:, hs], k[:, hs]), 0.0).astype(bf16)
        inner[h] = masked
        attn[:, hs] = nn(masked, v[:, hs])
        return carry

    lax.fori_loop(0, heads, inner_step, 0)

    onward_first = onward(0)
    exchanged(st_own, st_got, 0)

    def prefix_step(i, total):
        st_sum[piece_of(i), :] = total.astype(bf16)
        return total + st_got[piece_of(i), :].astype(f32)

    lax.fori_loop(0, n_ctx, prefix_step, jnp.zeros((share, DH), f32))
    exchange(st_sum, st_pre, 1)
    onward_second = onward(1)
    exchanged(st_sum, st_pre, 1)

    def norm_step(h, carry):
        hs = lanes(h)
        a = attn[:, hs] + nn(q[:, hs], st_pre[hs, :])
        r = lax.rsqrt(jnp.mean(a * a, axis=-1, keepdims=True) + 1e-06)
        x = a * r
        attn[:, hs] = x
        scale[h] = jnp.broadcast_to(r, x.shape)
        normed[:, hs] = (x * gain[:, hs]).astype(bf16)
        return carry

    lax.fori_loop(0, heads, norm_step, 0)

    loads[4].wait()

    def slab(owner):
        return pl.ds(pl.multiple_of(owner * rows, rows), rows)

    def columns(j):
        return pl.ds(pl.multiple_of(j * chunk, chunk), chunk)

    def relay(j, to):
        return pltpu.make_async_remote_copy(
            src_ref=p.at[slab(far), columns(j)],
            dst_ref=rel.at[:, columns(j)],
            send_sem=rel_send.at[j],
            recv_sem=rel_recv.at[j],
            device_id=(c, to),
            device_id_type=MESH,
        )

    def single(j, to, dst):
        return pltpu.make_async_remote_copy(
            src_ref=p.at[slab(to), columns(j)],
            dst_ref=dst.at[:, columns(j)],
            send_sem=one_send.at[j],
            recv_sem=one_recv.at[j],
            device_id=(c, to),
            device_id_type=MESH,
        )

    def double(j, to, dst):
        return pltpu.make_async_remote_copy(
            src_ref=rel.at[:, columns(j)],
            dst_ref=dst.at[:, columns(j)],
            send_sem=two_send.at[j],
            recv_sem=two_recv.at[j],
            device_id=(c, to),
            device_id_type=MESH,
        )

    n_half = n_chunk // 2

    def project(j):
        cs = columns(j)
        product = nn(normed[...], w[:, cs])
        part[...] = product
        p[:, cs] = product.astype(bf16)
        own[:, cs] = part[slab(y), :]

    def project_step(i, carry):
        project(i)
        relay(i, up).start()
        project(i + n_half)
        relay(i + n_half, down).start()
        return carry

    def single_step(i, carry):
        single(i, down, fin_up).start()
        single(i + n_half, up, fin_dn).start()
        return carry

    lax.fori_loop(0, n_half, project_step, 0)
    lax.fori_loop(0, n_half, single_step, 0)

    wide = 2 * DH

    def cot_columns(h):
        return cot[:, :, h * wing : (h + 1) * wing].reshape(tok, wing)

    def ng_first(i, carry):
        rs = pl.ds(pl.multiple_of(i * wide, wide), wide)
        ng[:, rs] = nt(cot_columns(0), w[rs, :wing])
        return carry

    def ng_second(i, carry):
        rs = pl.ds(pl.multiple_of(i * wide, wide), wide)
        ng[:, rs] += nt(cot_columns(1), w[rs, wing:])
        return carry

    loads[3].wait()
    for h in (ups[1], downs[1], *onward_first):
        h.wait_recv()
    lax.fori_loop(0, feat // wide, ng_first, 0)
    for h in (ups[3], downs[3], *onward_second):
        h.wait_recv()
    lax.fori_loop(0, feat // wide, ng_second, 0)

    def norm_back_step(h, carry):
        hs = lanes(h)
        x = attn[:, hs]
        g = ng[:, hs] * gain[:, hs]
        a = scale[h] * (g - x * jnp.mean(g * x, axis=-1, keepdims=True))
        a = a.astype(bf16)
        ag[:, hs] = a
        gs_own[hs, :] = tn(q[:, hs], a).astype(bf16)
        return carry

    lax.fori_loop(0, heads, norm_back_step, 0)
    exchange(gs_own, gs_got, 2)

    def grad_step(h, carry):
        hs = lanes(h)
        a = ag[:, hs]
        masked = jnp.where(causal, nt(a, v[:, hs]), 0.0).astype(bf16)
        dq[:, hs] = (nn(masked, k[:, hs]) + nt(a, st_pre[hs, :])).astype(bf16)
        dk[:, hs] = tn(masked, q[:, hs])
        dv[:, hs] = tn(inner[h], a)
        return carry

    lax.fori_loop(0, heads, grad_step, 0)

    def relay_step(i, carry):
        for j, src, to, dst in ((i, down, up, fin_dn), (i + n_half, up, down, fin_up)):
            cs = columns(j)
            relay(j, to).wait_recv()
            rel[:, cs] = (rel[:, cs].astype(f32) + p[slab(to), cs].astype(f32)).astype(bf16)
            double(j, to, dst).start()
        return carry

    lax.fori_loop(0, n_half - 1, relay_step, 0)

    exchanged(gs_own, gs_got, 2)

    def suffix_step(i, total):
        at = piece_of(n_ctx - 1 - i)
        gs_sum[at, :] = total.astype(bf16)
        return total + gs_got[at, :].astype(f32)

    lax.fori_loop(0, n_ctx, suffix_step, jnp.zeros((share, DH), f32))
    exchange(gs_sum, gs_suf, 3)

    relay_step(n_half - 1, 0)
    exchanged(gs_sum, gs_suf, 3)

    def last_step(h, carry):
        hs = lanes(h)
        dkb[:, hs] = (dk[:, hs] + nt(v[:, hs], gs_suf[hs, :])).astype(bf16)
        dvb[:, hs] = (dv[:, hs] + nn(k[:, hs], gs_suf[hs, :])).astype(bf16)
        return carry

    lax.fori_loop(0, heads, last_step, 0)

    def sum_step(i, carry):
        for j, to, one, two in ((i, down, fin_up, fin_dn), (i + n_half, up, fin_dn, fin_up)):
            cs = columns(j)
            single(j, to, one).wait_recv()
            double(j, to, two).wait_recv()
            lo[:, cs] = (
                own[:, cs] + (fin_dn[:, cs].astype(f32) + fin_up[:, cs].astype(f32))
            ).astype(bf16)
        return carry

    lax.fori_loop(0, n_half, sum_step, 0)

    for h in (*ups, *downs, *onward_first, *onward_second):
        h.wait_send()

    def sent_step(j, carry):
        relay(j, up).wait_send()
        single(j, up, fin_dn).wait_send()
        double(j, up, fin_dn).wait_send()
        return carry

    lax.fori_loop(0, n_chunk, sent_step, 0)


def store_kernel(*refs):
    sources, results, sem = refs[:4], refs[4:8], refs[8]
    copies = [
        pltpu.make_async_copy(src, dst, sem.at[i])
        for i, (src, dst) in enumerate(zip(sources, results))
    ]
    for copy in copies:
        copy.start()
    for copy in copies:
        copy.wait()


def per_device(n_ctx, n_head, queries, key_rows, value_rows, norm_gain, out_weight, out_cotangent):
    tok, feat = queries.shape
    rows, width = out_cotangent.shape
    heads = feat // DH
    chunk = width // 6
    n_chunk = width // chunk
    state = pltpu.VMEM((feat, DH), bf16)
    any_space = pl.BlockSpec(memory_space=pl.ANY)
    vmem = pl.BlockSpec(memory_space=pltpu.VMEM)
    dma = pltpu.SemaphoreType.DMA
    results = pl.pallas_call(
        functools.partial(kernel, n_ctx, n_head, chunk),
        out_shape=(
            pltpu.VMEM((rows, width), bf16),
            pltpu.VMEM((tok, feat), bf16),
            pltpu.VMEM((tok, feat), bf16),
            pltpu.VMEM((tok, feat), bf16),
        ),
        in_specs=[any_space, any_space, any_space, vmem, any_space, any_space],
        out_specs=(vmem, vmem, vmem, vmem),
        scratch_shapes=[
            pltpu.VMEM((tok, feat), bf16),
            pltpu.VMEM((tok, feat), bf16),
            pltpu.VMEM((tok, feat), bf16),
            pltpu.VMEM((feat, width), bf16),
            pltpu.VMEM((n_head, rows, width), bf16),
            pltpu.VMEM((heads, tok, tok), bf16),
            pltpu.VMEM((tok, feat), f32),
            pltpu.VMEM((heads, tok, DH), f32),
            pltpu.VMEM((tok, feat), bf16),
            pltpu.VMEM((tok, chunk), f32),
            pltpu.VMEM((rows, width), f32),
            pltpu.VMEM((tok, width), bf16),
            pltpu.VMEM((rows, width), bf16),
            pltpu.VMEM((rows, width), bf16),
            pltpu.VMEM((rows, width), bf16),
            pltpu.VMEM((tok, feat), f32),
            pltpu.VMEM((tok, feat), bf16),
            pltpu.VMEM((tok, feat), f32),
            pltpu.VMEM((tok, feat), f32),
            *[state] * 8,
            dma((5,)),
            pltpu.SemaphoreType.REGULAR,
            dma((12,)),
            dma((12,)),
            dma((4,)),
            dma((4,)),
            *[dma((n_chunk,))] * 6,
        ],
        compiler_params=pltpu.CompilerParams(
            collective_id=0, has_side_effects=True, vmem_limit_bytes=60 * 1024 * 1024
        ),
        cost_estimate=pl.CostEstimate(
            flops=8_000_000_000, bytes_accessed=18_000_000, transcendentals=0
        ),
    )(
        queries,
        key_rows,
        value_rows,
        norm_gain.reshape(1, feat),
        out_weight,
        out_cotangent,
    )
    return pl.pallas_call(
        store_kernel,
        out_shape=tuple(jax.ShapeDtypeStruct(r.shape, r.dtype) for r in results),
        in_specs=[vmem] * 4,
        out_specs=(any_space,) * 4,
        scratch_shapes=[dma((4,))],
        compiler_params=pltpu.CompilerParams(vmem_limit_bytes=1024 * 1024),
    )(*(pltpu.with_memory_space_constraint(r, pltpu.VMEM) for r in results))


def solution(mesh):
    in_specs = (
        P("ctx", "head"),
        P("ctx", "head"),
        P("ctx", "head"),
        P("head"),
        P("head", None),
        P(("ctx", "head"), None),
    )
    out_specs = (P(("ctx", "head"), None), P("ctx", "head"), P("ctx", "head"), P("ctx", "head"))
    return jax.shard_map(
        functools.partial(per_device, mesh.shape["ctx"], mesh.shape["head"]),
        mesh=mesh,
        in_specs=in_specs,
        out_specs=out_specs,
        check_vma=False,
    )
```

```python
import functools

import jax
import jax.numpy as jnp
from jax import lax
from jax.experimental import pallas as pl
from jax.experimental.pallas import tpu as pltpu
from jax.sharding import PartitionSpec as P

DH = 128
N_Z = 4
MESH = pl.DeviceIdType.MESH
f32 = jnp.float32
bf16 = jnp.bfloat16


def nn(a, b):
    return jnp.dot(a, b, preferred_element_type=f32)


def nt(a, b):
    return lax.dot_general(a, b, (((1,), (1,)), ((), ())), preferred_element_type=f32)


def tn(a, b):
    return lax.dot_general(a, b, (((0,), (0,)), ((), ())), preferred_element_type=f32)


def kernel(
    n_ctx,
    n_z,
    n_head,
    chunk,
    q_hbm,
    k_hbm,
    v_hbm,
    gain,
    w_hbm,
    cot_hbm,
    lo,
    dq,
    dkb,
    dvb,
    q,
    k,
    v,
    w,
    cot,
    inner,
    attn,
    scale,
    normed,
    part,
    own,
    p,
    rel,
    fin_dn,
    fin_up,
    ng,
    ag,
    dk,
    dv,
    st_own,
    st_got,
    st_sum,
    st_pre,
    gs_own,
    gs_got,
    gs_sum,
    gs_suf,
    ld_sem,
    ready,
    here,
    ag_send,
    ag_recv,
    sc_send,
    sc_recv,
    rel_send,
    rel_recv,
    one_send,
    one_recv,
    two_send,
    two_recv,
):
    c = lax.axis_index("ctx")
    y = lax.axis_index("head")
    up = lax.rem(y + 1, n_head)
    down = lax.rem(y + n_head - 1, n_head)
    far = lax.rem(y + 2, n_head)
    tok, feat = q.shape
    heads = feat // DH
    rows = cot.shape[1]
    width = cot.shape[2]
    n_chunk = width // chunk
    half = rows // 2
    wing = width // 2
    share = st_own.shape[0] // n_ctx

    loads = [
        pltpu.make_async_copy(src, dst, ld_sem.at[i])
        for i, (src, dst) in enumerate(
            ((k_hbm, k), (v_hbm, v), (q_hbm, q), (cot_hbm, cot.at[y]), (w_hbm, w))
        )
    ]
    for load in loads:
        load.start()

    barrier = pltpu.get_barrier_semaphore()
    n_group = n_ctx // n_z
    z, g = c // n_group, c % n_group

    def signal(sem, to):
        pl.semaphore_signal(sem, inc=1, device_id=(to, y), device_id_type=MESH)

    def greet_member(i, carry):
        signal(barrier, z * n_group + i)
        return carry

    def greet_line(i, carry):
        signal(barrier, i * n_group + g)
        return carry

    def answer_member(i, carry):
        signal(ready, z * n_group + i)
        return carry

    def answer_line(i, carry):
        signal(ready, i * n_group + g)
        return carry

    for near in (up, down):
        pl.semaphore_signal(barrier, inc=1, device_id=(c, near), device_id_type=MESH)
    lax.fori_loop(z + 1, n_z, greet_line, 0)
    lax.fori_loop(g + 1, n_group, greet_member, 0)
    pl.semaphore_wait(barrier, 2 + z + g)

    def quarter(r, h):
        return pl.ds(r * half, half), pl.ds(h * wing, wing)

    def hop(src, owner, r, h, to, i):
        return pltpu.make_async_remote_copy(
            src_ref=src.at[quarter(r, h)],
            dst_ref=cot.at[(owner, *quarter(r, h))],
            send_sem=ag_send.at[i],
            recv_sem=ag_recv.at[i],
            device_id=(c, to),
            device_id_type=MESH,
        )

    ups = [hop(cot_hbm, y, r, h, up, 2 * h + r) for h in (0, 1) for r in (0, 1)]
    downs = [hop(cot_hbm, y, 1 - r, h, down, 4 + 2 * h + r) for h in (0, 1) for r in (0, 1)]
    for one, other in zip(ups, downs):
        one.start()
        other.start()
    lax.fori_loop(0, z, answer_line, 0)
    lax.fori_loop(0, g, answer_member, 0)

    def onward(h):
        ups[2 * h].wait_recv()
        on_up = hop(cot.at[down], down, 0, h, up, 8 + h)
        on_up.start()
        downs[2 * h].wait_recv()
        on_down = hop(cot.at[up], up, 1, h, down, 10 + h)
        on_down.start()
        return on_up, on_down

    def lanes(h):
        return pl.ds(pl.multiple_of(h * DH, DH), DH)

    def piece_of(i):
        return pl.ds(pl.multiple_of(i * share, share), share)

    def exchange(src, dst, i):
        def step(j, carry):
            peer = lax.rem(c + 1 + lax.rem(j + n_ctx // 2, n_ctx - 1), n_ctx)
            pltpu.make_async_remote_copy(
                src_ref=src.at[piece_of(peer)],
                dst_ref=dst.at[piece_of(c)],
                send_sem=sc_send.at[i],
                recv_sem=sc_recv.at[i],
                device_id=(peer, y),
                device_id_type=MESH,
            ).start()
            return carry

        lax.fori_loop(1, n_ctx, step, 0)
        dst[piece_of(c), :] = src[piece_of(c), :]

    def exchanged(src, dst, i):
        whole = pl.ds(0, (n_ctx - 1) * share)
        all_of = pltpu.make_async_remote_copy(
            src_ref=src.at[whole],
            dst_ref=dst.at[whole],
            send_sem=sc_send.at[i],
            recv_sem=sc_recv.at[i],
            device_id=(lax.rem(c + 1, n_ctx), y),
            device_id_type=MESH,
        )
        all_of.wait_send()
        all_of.wait_recv()

    loads[0].wait()
    loads[1].wait()

    def state_step(h, carry):
        hs = lanes(h)
        st_own[hs, :] = tn(k[:, hs], v[:, hs]).astype(bf16)
        return carry

    lax.fori_loop(0, heads, state_step, 0)

    @pl.when(c < n_ctx - 1)
    def _():
        pl.semaphore_wait(ready, n_z - 1 - z + n_group - 1 - g)

    def tell_line(i, carry):
        signal(here, lax.rem(z + i, n_z) * n_group + g)
        return carry

    lax.fori_loop(1, n_z, tell_line, 0)
    pl.semaphore_wait(here, n_z - 1)

    exchange(st_own, st_got, 0)

    loads[2].wait()
    causal = lax.broadcasted_iota(jnp.int32, (tok, tok), 0) >= lax.broadcasted_iota(
        jnp.int32, (tok, tok), 1
    )

    def inner_step(h, carry):
        hs = lanes(h)
        masked = jnp.where(causal, nt(q[:, hs], k[:, hs]), 0.0).astype(bf16)
        inner[h] = masked
        attn[:, hs] = nn(masked, v[:, hs])
        return carry

    lax.fori_loop(0, heads, inner_step, 0)

    onward_first = onward(0)
    exchanged(st_own, st_got, 0)

    def prefix_step(i, total):
        st_sum[piece_of(i), :] = total.astype(bf16)
        return total + st_got[piece_of(i), :].astype(f32)

    lax.fori_loop(0, n_ctx, prefix_step, jnp.zeros((share, DH), f32))
    exchange(st_sum, st_pre, 1)
    onward_second = onward(1)
    exchanged(st_sum, st_pre, 1)

    def norm_step(h, carry):
        hs = lanes(h)
        a = attn[:, hs] + nn(q[:, hs], st_pre[hs, :])
        r = lax.rsqrt(jnp.mean(a * a, axis=-1, keepdims=True) + 1e-06)
        x = a * r
        attn[:, hs] = x
        scale[h] = jnp.broadcast_to(r, x.shape)
        normed[:, hs] = (x * gain[:, hs]).astype(bf16)
        return carry

    lax.fori_loop(0, heads, norm_step, 0)

    loads[4].wait()

    def slab(owner):
        return pl.ds(pl.multiple_of(owner * rows, rows), rows)

    def columns(j):
        return pl.ds(pl.multiple_of(j * chunk, chunk), chunk)

    def relay(j, to):
        return pltpu.make_async_remote_copy(
            src_ref=p.at[slab(far), columns(j)],
            dst_ref=rel.at[:, columns(j)],
            send_sem=rel_send.at[j],
            recv_sem=rel_recv.at[j],
            device_id=(c, to),
            device_id_type=MESH,
        )

    def single(j, to, dst):
        return pltpu.make_async_remote_copy(
            src_ref=p.at[slab(to), columns(j)],
            dst_ref=dst.at[:, columns(j)],
            send_sem=one_send.at[j],
            recv_sem=one_recv.at[j],
            device_id=(c, to),
            device_id_type=MESH,
        )

    def double(j, to, dst):
        return pltpu.make_async_remote_copy(
            src_ref=rel.at[:, columns(j)],
            dst_ref=dst.at[:, columns(j)],
            send_sem=two_send.at[j],
            recv_sem=two_recv.at[j],
            device_id=(c, to),
            device_id_type=MESH,
        )

    n_half = n_chunk // 2

    def project(j):
        cs = columns(j)
        product = nn(normed[...], w[:, cs])
        part[...] = product
        p[:, cs] = product.astype(bf16)
        own[:, cs] = part[slab(y), :]

    def project_step(i, carry):
        project(i)
        relay(i, up).start()
        project(i + n_half)
        relay(i + n_half, down).start()
        return carry

    def single_step(i, carry):
        single(i, down, fin_up).start()
        single(i + n_half, up, fin_dn).start()
        return carry

    lax.fori_loop(0, n_half, project_step, 0)
    lax.fori_loop(0, n_half, single_step, 0)

    wide = 2 * DH

    def cot_columns(h):
        return cot[:, :, h * wing : (h + 1) * wing].reshape(tok, wing)

    def ng_first(i, carry):
        rs = pl.ds(pl.multiple_of(i * wide, wide), wide)
        ng[:, rs] = nt(cot_columns(0), w[rs, :wing])
        return carry

    def ng_second(i, carry):
        rs = pl.ds(pl.multiple_of(i * wide, wide), wide)
        ng[:, rs] += nt(cot_columns(1), w[rs, wing:])
        return carry

    loads[3].wait()
    for h in (ups[1], downs[1], *onward_first):
        h.wait_recv()
    lax.fori_loop(0, feat // wide, ng_first, 0)
    for h in (ups[3], downs[3], *onward_second):
        h.wait_recv()
    lax.fori_loop(0, feat // wide, ng_second, 0)

    def norm_back_step(h, carry):
        hs = lanes(h)
        x = attn[:, hs]
        g = ng[:, hs] * gain[:, hs]
        a = scale[h] * (g - x * jnp.mean(g * x, axis=-1, keepdims=True))
        a = a.astype(bf16)
        ag[:, hs] = a
        gs_own[hs, :] = tn(q[:, hs], a).astype(bf16)
        return carry

    lax.fori_loop(0, heads, norm_back_step, 0)
    exchange(gs_own, gs_got, 2)

    def grad_step(h, carry):
        hs = lanes(h)
        a = ag[:, hs]
        masked = jnp.where(causal, nt(a, v[:, hs]), 0.0).astype(bf16)
        dq[:, hs] = (nn(masked, k[:, hs]) + nt(a, st_pre[hs, :])).astype(bf16)
        dk[:, hs] = tn(masked, q[:, hs])
        dv[:, hs] = tn(inner[h], a)
        return carry

    lax.fori_loop(0, heads, grad_step, 0)

    def relay_step(i, carry):
        for j, src, to, dst in ((i, down, up, fin_dn), (i + n_half, up, down, fin_up)):
            cs = columns(j)
            relay(j, to).wait_recv()
            rel[:, cs] = (rel[:, cs].astype(f32) + p[slab(to), cs].astype(f32)).astype(bf16)
            double(j, to, dst).start()
        return carry

    lax.fori_loop(0, n_half - 1, relay_step, 0)

    exchanged(gs_own, gs_got, 2)

    def suffix_step(i, total):
        at = piece_of(n_ctx - 1 - i)
        gs_sum[at, :] = total.astype(bf16)
        return total + gs_got[at, :].astype(f32)

    lax.fori_loop(0, n_ctx, suffix_step, jnp.zeros((share, DH), f32))
    exchange(gs_sum, gs_suf, 3)

    relay_step(n_half - 1, 0)
    exchanged(gs_sum, gs_suf, 3)

    def last_step(h, carry):
        hs = lanes(h)
        dkb[:, hs] = (dk[:, hs] + nt(v[:, hs], gs_suf[hs, :])).astype(bf16)
        dvb[:, hs] = (dv[:, hs] + nn(k[:, hs], gs_suf[hs, :])).astype(bf16)
        return carry

    lax.fori_loop(0, heads, last_step, 0)

    def sum_step(i, carry):
        for j, to, one, two in ((i, down, fin_up, fin_dn), (i + n_half, up, fin_dn, fin_up)):
            cs = columns(j)
            single(j, to, one).wait_recv()
            double(j, to, two).wait_recv()
            lo[:, cs] = (
                own[:, cs] + (fin_dn[:, cs].astype(f32) + fin_up[:, cs].astype(f32))
            ).astype(bf16)
        return carry

    lax.fori_loop(0, n_half, sum_step, 0)

    for h in (*ups, *downs, *onward_first, *onward_second):
        h.wait_send()

    def sent_step(j, carry):
        relay(j, up).wait_send()
        single(j, up, fin_dn).wait_send()
        double(j, up, fin_dn).wait_send()
        return carry

    lax.fori_loop(0, n_chunk, sent_step, 0)


def store_kernel(*refs):
    sources, results, sem = refs[:4], refs[4:8], refs[8]
    copies = [
        pltpu.make_async_copy(src, dst, sem.at[i])
        for i, (src, dst) in enumerate(zip(sources, results))
    ]
    for copy in copies:
        copy.start()
    for copy in copies:
        copy.wait()


def per_device(n_ctx, n_z, n_head, queries, key_rows, value_rows, norm_gain, out_weight, out_cotangent):
    tok, feat = queries.shape
    rows, width = out_cotangent.shape
    heads = feat // DH
    chunk = width // 6
    n_chunk = width // chunk
    state = pltpu.VMEM((feat, DH), bf16)
    any_space = pl.BlockSpec(memory_space=pl.ANY)
    vmem = pl.BlockSpec(memory_space=pltpu.VMEM)
    dma = pltpu.SemaphoreType.DMA
    results = pl.pallas_call(
        functools.partial(kernel, n_ctx, n_z, n_head, chunk),
        out_shape=(
            pltpu.VMEM((rows, width), bf16),
            pltpu.VMEM((tok, feat), bf16),
            pltpu.VMEM((tok, feat), bf16),
            pltpu.VMEM((tok, feat), bf16),
        ),
        in_specs=[any_space, any_space, any_space, vmem, any_space, any_space],
        out_specs=(vmem, vmem, vmem, vmem),
        scratch_shapes=[
            pltpu.VMEM((tok, feat), bf16),
            pltpu.VMEM((tok, feat), bf16),
            pltpu.VMEM((tok, feat), bf16),
            pltpu.VMEM((feat, width), bf16),
            pltpu.VMEM((n_head, rows, width), bf16),
            pltpu.VMEM((heads, tok, tok), bf16),
            pltpu.VMEM((tok, feat), f32),
            pltpu.VMEM((heads, tok, DH), f32),
            pltpu.VMEM((tok, feat), bf16),
            pltpu.VMEM((tok, chunk), f32),
            pltpu.VMEM((rows, width), f32),
            pltpu.VMEM((tok, width), bf16),
            pltpu.VMEM((rows, width), bf16),
            pltpu.VMEM((rows, width), bf16),
            pltpu.VMEM((rows, width), bf16),
            pltpu.VMEM((tok, feat), f32),
            pltpu.VMEM((tok, feat), bf16),
            pltpu.VMEM((tok, feat), f32),
            pltpu.VMEM((tok, feat), f32),
            *[state] * 8,
            dma((5,)),
            pltpu.SemaphoreType.REGULAR,
            pltpu.SemaphoreType.REGULAR,
            dma((12,)),
            dma((12,)),
            dma((4,)),
            dma((4,)),
            *[dma((n_chunk,))] * 6,
        ],
        compiler_params=pltpu.CompilerParams(
            collective_id=0, has_side_effects=True, vmem_limit_bytes=60 * 1024 * 1024
        ),
        cost_estimate=pl.CostEstimate(
            flops=8_000_000_000, bytes_accessed=18_000_000, transcendentals=0
        ),
    )(
        queries,
        key_rows,
        value_rows,
        norm_gain.reshape(1, feat),
        out_weight,
        out_cotangent,
    )
    return pl.pallas_call(
        store_kernel,
        out_shape=tuple(jax.ShapeDtypeStruct(r.shape, r.dtype) for r in results),
        in_specs=[vmem] * 4,
        out_specs=(any_space,) * 4,
        scratch_shapes=[dma((4,))],
        compiler_params=pltpu.CompilerParams(vmem_limit_bytes=1024 * 1024),
    )(*(pltpu.with_memory_space_constraint(r, pltpu.VMEM) for r in results))


def solution(mesh):
    in_specs = (
        P("ctx", "head"),
        P("ctx", "head"),
        P("ctx", "head"),
        P("head"),
        P("head", None),
        P(("ctx", "head"), None),
    )
    out_specs = (P(("ctx", "head"), None), P("ctx", "head"), P("ctx", "head"), P("ctx", "head"))
    return jax.shard_map(
        functools.partial(per_device, mesh.shape["ctx"], N_Z, mesh.shape["head"]),
        mesh=mesh,
        in_specs=in_specs,
        out_specs=out_specs,
        check_vma=False,
    )
```

```python
import functools

import jax
import jax.numpy as jnp
from jax import lax
from jax.experimental import pallas as pl
from jax.experimental.pallas import tpu as pltpu
from jax.sharding import PartitionSpec as P

DH = 128
N_STORE = 4
N_Z = 4
MESH = pl.DeviceIdType.MESH
f32 = jnp.float32
bf16 = jnp.bfloat16


def nn(a, b):
    return jnp.dot(a, b, preferred_element_type=f32)


def nt(a, b):
    return lax.dot_general(a, b, (((1,), (1,)), ((), ())), preferred_element_type=f32)


def tn(a, b):
    return lax.dot_general(a, b, (((0,), (0,)), ((), ())), preferred_element_type=f32)


def kernel(
    n_ctx,
    n_z,
    n_head,
    chunk,
    q_hbm,
    k_hbm,
    v_hbm,
    gain,
    w_hbm,
    cot_hbm,
    lo,
    dq,
    dkb,
    dvb,
    q,
    k,
    v,
    w,
    cot,
    inner,
    attn,
    scale,
    normed,
    part,
    own,
    p,
    rel,
    fin_dn,
    fin_up,
    ng,
    ag,
    dk,
    dv,
    st_own,
    st_got,
    st_sum,
    st_pre,
    gs_own,
    gs_got,
    gs_sum,
    gs_suf,
    ld_sem,
    ready,
    here,
    ag_send,
    ag_recv,
    sc_send,
    sc_recv,
    rel_send,
    rel_recv,
    one_send,
    one_recv,
    two_send,
    two_recv,
):
    c = lax.axis_index("ctx")
    y = lax.axis_index("head")
    up = lax.rem(y + 1, n_head)
    down = lax.rem(y + n_head - 1, n_head)
    far = lax.rem(y + 2, n_head)
    tok, feat = q.shape
    heads = feat // DH
    rows = cot.shape[1]
    width = cot.shape[2]
    n_chunk = width // chunk
    half = rows // 2
    wing = width // 2
    share = st_own.shape[0] // n_ctx

    loads = [
        pltpu.make_async_copy(src, dst, ld_sem.at[i])
        for i, (src, dst) in enumerate(
            ((k_hbm, k), (v_hbm, v), (q_hbm, q), (cot_hbm, cot.at[y]), (w_hbm, w))
        )
    ]
    barrier = pltpu.get_barrier_semaphore()
    n_group = n_ctx // n_z
    z, g = c // n_group, c % n_group

    def ranked(i):
        x = i // 2
        return 2 * (x + (x // 2) * (1 - 2 * (x % 2))) + i % 2

    rank = ranked(g)

    def signal(sem, to):
        pl.semaphore_signal(sem, inc=1, device_id=(to, y), device_id_type=MESH)

    def greet_member(i, carry):
        signal(barrier, z * n_group + ranked(i))
        return carry

    def greet_line(i, carry):
        signal(barrier, i * n_group + g)
        return carry

    def answer_member(i, carry):
        signal(ready, z * n_group + ranked(i))
        return carry

    def answer_line(i, carry):
        signal(ready, i * n_group + g)
        return carry

    for near in (up, down):
        pl.semaphore_signal(barrier, inc=1, device_id=(c, near), device_id_type=MESH)
    lax.fori_loop(z + 1, n_z, greet_line, 0)
    lax.fori_loop(rank + 1, n_group, greet_member, 0)
    for i in (3, 0, 1, 2, 4):
        loads[i].start()
    loads[3].wait()
    pl.semaphore_wait(barrier, 2 + z + rank)

    def portion(r, h):
        return pl.ds(*r), pl.ds(h * wing, wing)

    every, upper, lower = (0, rows), (0, half), (half, half)

    def hop(src, owner, r, h, to, i):
        return pltpu.make_async_remote_copy(
            src_ref=src.at[portion(r, h)],
            dst_ref=cot.at[(owner, *portion(r, h))],
            send_sem=ag_send.at[i],
            recv_sem=ag_recv.at[i],
            device_id=(c, to),
            device_id_type=MESH,
        )

    ups = [hop(cot.at[y], y, every, h, up, h) for h in (0, 1)]
    downs = [hop(cot.at[y], y, every, h, down, 2 + h) for h in (0, 1)]
    for one, other in zip(ups, downs):
        one.start()
        other.start()
    lax.fori_loop(0, z, answer_line, 0)
    lax.fori_loop(0, rank, answer_member, 0)

    def onward(h):
        ups[h].wait_recv()
        on_up = hop(cot.at[down], down, upper, h, up, 4 + h)
        on_up.start()
        downs[h].wait_recv()
        on_down = hop(cot.at[up], up, lower, h, down, 6 + h)
        on_down.start()
        return on_up, on_down

    def lanes(h):
        return pl.ds(pl.multiple_of(h * DH, DH), DH)

    def piece_of(i):
        return pl.ds(pl.multiple_of(i * share, share), share)

    def exchange(src, dst, i):
        def step(j, carry):
            peer = lax.rem(c + 1 + lax.rem(j + n_ctx // 2, n_ctx - 1), n_ctx)
            pltpu.make_async_remote_copy(
                src_ref=src.at[piece_of(peer)],
                dst_ref=dst.at[piece_of(c)],
                send_sem=sc_send.at[i],
                recv_sem=sc_recv.at[i],
                device_id=(peer, y),
                device_id_type=MESH,
            ).start()
            return carry

        lax.fori_loop(1, n_ctx, step, 0)
        dst[piece_of(c), :] = src[piece_of(c), :]

    def exchanged(src, dst, i):
        whole = pl.ds(0, (n_ctx - 1) * share)
        all_of = pltpu.make_async_remote_copy(
            src_ref=src.at[whole],
            dst_ref=dst.at[whole],
            send_sem=sc_send.at[i],
            recv_sem=sc_recv.at[i],
            device_id=(lax.rem(c + 1, n_ctx), y),
            device_id_type=MESH,
        )
        all_of.wait_send()
        all_of.wait_recv()

    loads[0].wait()
    loads[1].wait()

    def state_step(h, carry):
        hs = lanes(h)
        st_own[hs, :] = tn(k[:, hs], v[:, hs]).astype(bf16)
        return carry

    lax.fori_loop(0, heads, state_step, 0)

    @pl.when(n_z - 1 - z + n_group - 1 - rank > 0)
    def _():
        pl.semaphore_wait(ready, n_z - 1 - z + n_group - 1 - rank)

    def tell_line(i, carry):
        signal(here, lax.rem(z + i, n_z) * n_group + g)
        return carry

    lax.fori_loop(1, n_z, tell_line, 0)
    pl.semaphore_wait(here, n_z - 1)

    exchange(st_own, st_got, 0)

    loads[2].wait()
    causal = lax.broadcasted_iota(jnp.int32, (tok, tok), 0) >= lax.broadcasted_iota(
        jnp.int32, (tok, tok), 1
    )

    def inner_step(h, carry):
        hs = lanes(h)
        masked = jnp.where(causal, nt(q[:, hs], k[:, hs]), 0.0).astype(bf16)
        inner[h] = masked
        attn[:, hs] = nn(masked, v[:, hs])
        return carry

    lax.fori_loop(0, heads, inner_step, 0)

    onward_first = onward(0)
    exchanged(st_own, st_got, 0)

    def prefix_step(i, total):
        st_sum[piece_of(i), :] = total.astype(bf16)
        return total + st_got[piece_of(i), :].astype(f32)

    lax.fori_loop(0, n_ctx, prefix_step, jnp.zeros((share, DH), f32))
    exchange(st_sum, st_pre, 1)
    onward_second = onward(1)
    exchanged(st_sum, st_pre, 1)

    def norm_step(h, carry):
        hs = lanes(h)
        a = attn[:, hs] + nn(q[:, hs], st_pre[hs, :])
        r = lax.rsqrt(jnp.mean(a * a, axis=-1, keepdims=True) + 1e-06)
        x = a * r
        attn[:, hs] = x
        scale[h] = jnp.broadcast_to(r, x.shape)
        normed[:, hs] = (x * gain[:, hs]).astype(bf16)
        return carry

    lax.fori_loop(0, heads, norm_step, 0)

    loads[4].wait()

    def slab(owner):
        return pl.ds(pl.multiple_of(owner * rows, rows), rows)

    def columns(j):
        return pl.ds(pl.multiple_of(j * chunk, chunk), chunk)

    def relay(j, to):
        return pltpu.make_async_remote_copy(
            src_ref=p.at[slab(far), columns(j)],
            dst_ref=rel.at[:, columns(j)],
            send_sem=rel_send.at[j],
            recv_sem=rel_recv.at[j],
            device_id=(c, to),
            device_id_type=MESH,
        )

    def single(h, to, dst):
        cs = pl.ds(h * wing, wing)
        return pltpu.make_async_remote_copy(
            src_ref=p.at[slab(to), cs],
            dst_ref=dst.at[:, cs],
            send_sem=one_send.at[h],
            recv_sem=one_recv.at[h],
            device_id=(c, to),
            device_id_type=MESH,
        )

    def double(j, to, dst):
        return pltpu.make_async_remote_copy(
            src_ref=rel.at[:, columns(j)],
            dst_ref=dst.at[:, columns(j)],
            send_sem=two_send.at[j],
            recv_sem=two_recv.at[j],
            device_id=(c, to),
            device_id_type=MESH,
        )

    n_half = n_chunk // 2

    def project(j):
        cs = columns(j)
        product = nn(normed[...], w[:, cs])
        part[...] = product
        p[:, cs] = product.astype(bf16)
        own[:, cs] = part[slab(y), :]

    def project_step(i, carry):
        project(i)
        relay(i, up).start()
        project(i + n_half)
        relay(i + n_half, down).start()
        return carry

    lax.fori_loop(0, n_half, project_step, 0)
    single(0, down, fin_up).start()
    single(1, up, fin_dn).start()

    wide = 2 * DH

    def cot_columns(h):
        return cot[:, :, h * wing : (h + 1) * wing].reshape(tok, wing)

    def ng_first(i, carry):
        rs = pl.ds(pl.multiple_of(i * wide, wide), wide)
        ng[:, rs] = nt(cot_columns(0), w[rs, :wing])
        return carry

    def ng_second(i, carry):
        rs = pl.ds(pl.multiple_of(i * wide, wide), wide)
        ng[:, rs] += nt(cot_columns(1), w[rs, wing:])
        return carry

    for h in onward_first:
        h.wait_recv()
    lax.fori_loop(0, feat // wide, ng_first, 0)
    for h in onward_second:
        h.wait_recv()
    lax.fori_loop(0, feat // wide, ng_second, 0)

    def norm_back_step(h, carry):
        hs = lanes(h)
        x = attn[:, hs]
        g = ng[:, hs] * gain[:, hs]
        a = scale[h] * (g - x * jnp.mean(g * x, axis=-1, keepdims=True))
        a = a.astype(bf16)
        ag[:, hs] = a
        gs_own[hs, :] = tn(q[:, hs], a).astype(bf16)
        return carry

    lax.fori_loop(0, heads, norm_back_step, 0)
    exchange(gs_own, gs_got, 2)

    def grad_step(h, carry):
        hs = lanes(h)
        a = ag[:, hs]
        masked = jnp.where(causal, nt(a, v[:, hs]), 0.0).astype(bf16)
        dq[:, hs] = (nn(masked, k[:, hs]) + nt(a, st_pre[hs, :])).astype(bf16)
        dk[:, hs] = tn(masked, q[:, hs])
        dv[:, hs] = tn(inner[h], a)
        return carry

    lax.fori_loop(0, heads, grad_step, 0)

    def relay_step(i, carry):
        for j, src, to, dst in ((i, down, up, fin_dn), (i + n_half, up, down, fin_up)):
            cs = columns(j)
            relay(j, to).wait_recv()
            rel[:, cs] = (rel[:, cs].astype(f32) + p[slab(to), cs].astype(f32)).astype(bf16)
            double(j, to, dst).start()
        return carry

    lax.fori_loop(0, n_half - 1, relay_step, 0)

    exchanged(gs_own, gs_got, 2)

    def suffix_step(i, total):
        at = piece_of(n_ctx - 1 - i)
        gs_sum[at, :] = total.astype(bf16)
        return total + gs_got[at, :].astype(f32)

    lax.fori_loop(0, n_ctx, suffix_step, jnp.zeros((share, DH), f32))
    exchange(gs_sum, gs_suf, 3)

    relay_step(n_half - 1, 0)
    exchanged(gs_sum, gs_suf, 3)

    def last_step(h, carry):
        hs = lanes(h)
        dkb[:, hs] = (dk[:, hs] + nt(v[:, hs], gs_suf[hs, :])).astype(bf16)
        dvb[:, hs] = (dv[:, hs] + nn(k[:, hs], gs_suf[hs, :])).astype(bf16)
        return carry

    lax.fori_loop(0, heads, last_step, 0)

    def sum_step(i, carry):
        for j, to, two in ((i, down, fin_dn), (i + n_half, up, fin_up)):
            cs = columns(j)
            double(j, to, two).wait_recv()
            lo[:, cs] = (
                own[:, cs] + (fin_dn[:, cs].astype(f32) + fin_up[:, cs].astype(f32))
            ).astype(bf16)
        return carry

    single(0, down, fin_up).wait_recv()
    single(1, up, fin_dn).wait_recv()
    lax.fori_loop(0, n_half, sum_step, 0)

    for h in (*ups, *downs, *onward_first, *onward_second):
        h.wait_send()

    single(0, down, fin_up).wait_send()
    single(1, up, fin_dn).wait_send()

    def sent_step(j, carry):
        relay(j, up).wait_send()
        double(j, up, fin_dn).wait_send()
        return carry

    lax.fori_loop(0, n_chunk, sent_step, 0)


def store_kernel(*refs):
    sources, results, sem = refs[:4], refs[4:8], refs[8]
    copies = []
    for src, dst in zip(sources, results):
        step = src.shape[0] // N_STORE
        for piece in (pl.ds(i * step, step) for i in range(N_STORE)):
            copies.append(
                pltpu.make_async_copy(src.at[piece], dst.at[piece], sem.at[len(copies)])
            )
    for copy in copies:
        copy.start()
    for copy in copies:
        copy.wait()


def per_device(n_ctx, n_z, n_head, queries, key_rows, value_rows, norm_gain, out_weight, out_cotangent):
    tok, feat = queries.shape
    rows, width = out_cotangent.shape
    heads = feat // DH
    chunk = width // 6
    n_chunk = width // chunk
    state = pltpu.VMEM((feat, DH), bf16)
    any_space = pl.BlockSpec(memory_space=pl.ANY)
    vmem = pl.BlockSpec(memory_space=pltpu.VMEM)
    dma = pltpu.SemaphoreType.DMA
    results = pl.pallas_call(
        functools.partial(kernel, n_ctx, n_z, n_head, chunk),
        out_shape=(
            pltpu.VMEM((rows, width), bf16),
            pltpu.VMEM((tok, feat), bf16),
            pltpu.VMEM((tok, feat), bf16),
            pltpu.VMEM((tok, feat), bf16),
        ),
        in_specs=[any_space, any_space, any_space, vmem, any_space, any_space],
        out_specs=(vmem, vmem, vmem, vmem),
        scratch_shapes=[
            pltpu.VMEM((tok, feat), bf16),
            pltpu.VMEM((tok, feat), bf16),
            pltpu.VMEM((tok, feat), bf16),
            pltpu.VMEM((feat, width), bf16),
            pltpu.VMEM((n_head, rows, width), bf16),
            pltpu.VMEM((heads, tok, tok), bf16),
            pltpu.VMEM((tok, feat), f32),
            pltpu.VMEM((heads, tok, DH), f32),
            pltpu.VMEM((tok, feat), bf16),
            pltpu.VMEM((tok, chunk), f32),
            pltpu.VMEM((rows, width), f32),
            pltpu.VMEM((tok, width), bf16),
            pltpu.VMEM((rows, width), bf16),
            pltpu.VMEM((rows, width), bf16),
            pltpu.VMEM((rows, width), bf16),
            pltpu.VMEM((tok, feat), f32),
            pltpu.VMEM((tok, feat), bf16),
            pltpu.VMEM((tok, feat), f32),
            pltpu.VMEM((tok, feat), f32),
            *[state] * 8,
            dma((5,)),
            pltpu.SemaphoreType.REGULAR,
            pltpu.SemaphoreType.REGULAR,
            dma((8,)),
            dma((8,)),
            dma((4,)),
            dma((4,)),
            *[dma((n_chunk,))] * 6,
        ],
        compiler_params=pltpu.CompilerParams(
            collective_id=0, has_side_effects=True, vmem_limit_bytes=60 * 1024 * 1024
        ),
        cost_estimate=pl.CostEstimate(
            flops=8_000_000_000, bytes_accessed=18_000_000, transcendentals=0
        ),
    )(
        queries,
        key_rows,
        value_rows,
        norm_gain.reshape(1, feat),
        out_weight,
        out_cotangent,
    )
    return pl.pallas_call(
        store_kernel,
        out_shape=tuple(jax.ShapeDtypeStruct(r.shape, r.dtype) for r in results),
        in_specs=[vmem] * 4,
        out_specs=(any_space,) * 4,
        scratch_shapes=[dma((4 * N_STORE,))],
        compiler_params=pltpu.CompilerParams(vmem_limit_bytes=1024 * 1024),
    )(*(pltpu.with_memory_space_constraint(r, pltpu.VMEM) for r in results))


def solution(mesh):
    in_specs = (
        P("ctx", "head"),
        P("ctx", "head"),
        P("ctx", "head"),
        P("head"),
        P("head", None),
        P(("ctx", "head"), None),
    )
    out_specs = (P(("ctx", "head"), None), P("ctx", "head"), P("ctx", "head"), P("ctx", "head"))
    return jax.shard_map(
        functools.partial(per_device, mesh.shape["ctx"], N_Z, mesh.shape["head"]),
        mesh=mesh,
        in_specs=in_specs,
        out_specs=out_specs,
        check_vma=False,
    )
```

```python
import functools

import jax
import jax.numpy as jnp
from jax import lax
from jax.experimental import pallas as pl
from jax.experimental.pallas import tpu as pltpu
from jax.sharding import PartitionSpec as P

DH = 128
N_STORE = 4
N_Z = 4
MESH = pl.DeviceIdType.MESH
f32 = jnp.float32
bf16 = jnp.bfloat16


def nn(a, b):
    return jnp.dot(a, b, preferred_element_type=f32)


def nt(a, b):
    return lax.dot_general(a, b, (((1,), (1,)), ((), ())), preferred_element_type=f32)


def tn(a, b):
    return lax.dot_general(a, b, (((0,), (0,)), ((), ())), preferred_element_type=f32)


def kernel(
    n_ctx,
    n_z,
    n_head,
    chunk,
    q_hbm,
    k_hbm,
    v_hbm,
    gain,
    w_hbm,
    cot_hbm,
    lo,
    dq,
    dkb,
    dvb,
    q,
    k,
    v,
    w,
    cot,
    inner,
    attn,
    scale,
    normed,
    part,
    own,
    p,
    rel,
    fin_dn,
    fin_up,
    ng,
    ag,
    dk,
    dv,
    st_own,
    st_got,
    st_sum,
    st_pre,
    gs_own,
    gs_got,
    gs_sum,
    gs_suf,
    ld_sem,
    ready,
    here,
    ag_send,
    ag_recv,
    sc_send,
    sc_recv,
    rel_send,
    rel_recv,
    one_send,
    one_recv,
    two_send,
    two_recv,
):
    c = lax.axis_index("ctx")
    y = lax.axis_index("head")
    up = lax.rem(y + 1, n_head)
    down = lax.rem(y + n_head - 1, n_head)
    far = lax.rem(y + 2, n_head)
    tok, feat = q.shape
    heads = feat // DH
    rows = cot.shape[1]
    width = cot.shape[2]
    n_chunk = width // chunk
    half = rows // 2
    wing = width // 2
    share = st_own.shape[0] // n_ctx

    loads = [
        pltpu.make_async_copy(src, dst, ld_sem.at[i])
        for i, (src, dst) in enumerate(
            ((k_hbm, k), (v_hbm, v), (q_hbm, q), (cot_hbm, cot.at[y]), (w_hbm, w))
        )
    ]
    barrier = pltpu.get_barrier_semaphore()
    n_group = n_ctx // n_z
    z, g = c // n_group, c % n_group

    def ranked(i):
        x = i // 2
        return 2 * (x + (x // 2) * (1 - 2 * (x % 2))) + i % 2

    rank = ranked(g)

    def signal(sem, to):
        pl.semaphore_signal(sem, inc=1, device_id=(to, y), device_id_type=MESH)

    def greet_member(i, carry):
        signal(barrier, z * n_group + ranked(i))
        return carry

    def greet_line(i, carry):
        signal(barrier, i * n_group + g)
        return carry

    def answer_member(i, carry):
        signal(ready, z * n_group + ranked(i))
        return carry

    def answer_line(i, carry):
        signal(ready, i * n_group + g)
        return carry

    for near in (up, down):
        pl.semaphore_signal(barrier, inc=1, device_id=(c, near), device_id_type=MESH)
    lax.fori_loop(z + 1, n_z, greet_line, 0)
    lax.fori_loop(rank + 1, n_group, greet_member, 0)
    for i in (3, 0, 1, 2, 4):
        loads[i].start()
    loads[3].wait()
    pl.semaphore_wait(barrier, 2 + z + rank)

    def portion(r, h):
        return pl.ds(*r), pl.ds(h * wing, wing)

    every, upper, lower = (0, rows), (0, half), (half, half)

    def hop(src, owner, r, h, to, i):
        return pltpu.make_async_remote_copy(
            src_ref=src.at[portion(r, h)],
            dst_ref=cot.at[(owner, *portion(r, h))],
            send_sem=ag_send.at[i],
            recv_sem=ag_recv.at[i],
            device_id=(c, to),
            device_id_type=MESH,
        )

    ups = [hop(cot.at[y], y, every, h, up, h) for h in (0, 1)]
    downs = [hop(cot.at[y], y, every, h, down, 2 + h) for h in (0, 1)]
    for one, other in zip(ups, downs):
        one.start()
        other.start()
    lax.fori_loop(0, z, answer_line, 0)
    lax.fori_loop(0, rank, answer_member, 0)

    def onward(h):
        ups[h].wait_recv()
        on_up = hop(cot.at[down], down, upper, h, up, 4 + h)
        on_up.start()
        downs[h].wait_recv()
        on_down = hop(cot.at[up], up, lower, h, down, 6 + h)
        on_down.start()
        return on_up, on_down

    def lanes(h):
        return pl.ds(pl.multiple_of(h * DH, DH), DH)

    def piece_of(i):
        return pl.ds(pl.multiple_of(i * share, share), share)

    def exchange(src, dst, i):
        def step(j, carry):
            peer = lax.rem(c + 1 + lax.rem(j + n_ctx // 2, n_ctx - 1), n_ctx)
            pltpu.make_async_remote_copy(
                src_ref=src.at[piece_of(peer)],
                dst_ref=dst.at[piece_of(c)],
                send_sem=sc_send.at[i],
                recv_sem=sc_recv.at[i],
                device_id=(peer, y),
                device_id_type=MESH,
            ).start()
            return carry

        lax.fori_loop(1, n_ctx, step, 0)
        dst[piece_of(c), :] = src[piece_of(c), :]

    def exchanged(src, dst, i):
        whole = pl.ds(0, (n_ctx - 1) * share)
        all_of = pltpu.make_async_remote_copy(
            src_ref=src.at[whole],
            dst_ref=dst.at[whole],
            send_sem=sc_send.at[i],
            recv_sem=sc_recv.at[i],
            device_id=(lax.rem(c + 1, n_ctx), y),
            device_id_type=MESH,
        )
        all_of.wait_send()
        all_of.wait_recv()

    loads[0].wait()
    loads[1].wait()

    def state_step(h, carry):
        hs = lanes(h)
        st_own[hs, :] = tn(k[:, hs], v[:, hs]).astype(bf16)
        return carry

    lax.fori_loop(0, heads, state_step, 0)

    @pl.when(n_z - 1 - z + n_group - 1 - rank > 0)
    def _():
        pl.semaphore_wait(ready, n_z - 1 - z + n_group - 1 - rank)

    def tell_line(i, carry):
        signal(here, lax.rem(z + i, n_z) * n_group + g)
        return carry

    lax.fori_loop(1, n_z, tell_line, 0)
    pl.semaphore_wait(here, n_z - 1)

    exchange(st_own, st_got, 0)

    loads[2].wait()
    causal = lax.broadcasted_iota(jnp.int32, (tok, tok), 0) >= lax.broadcasted_iota(
        jnp.int32, (tok, tok), 1
    )

    def inner_step(h, carry):
        hs = lanes(h)
        masked = jnp.where(causal, nt(q[:, hs], k[:, hs]), 0.0).astype(bf16)
        inner[h] = masked
        attn[:, hs] = nn(masked, v[:, hs])
        return carry

    lax.fori_loop(0, heads, inner_step, 0)

    onward_first = onward(0)
    exchanged(st_own, st_got, 0)

    def prefix_step(i, total):
        st_sum[piece_of(i), :] = total.astype(bf16)
        return total + st_got[piece_of(i), :].astype(f32)

    lax.fori_loop(0, n_ctx, prefix_step, jnp.zeros((share, DH), f32))
    exchange(st_sum, st_pre, 1)
    onward_second = onward(1)
    exchanged(st_sum, st_pre, 1)

    def norm_step(h, carry):
        hs = lanes(h)
        a = attn[:, hs] + nn(q[:, hs], st_pre[hs, :])
        r = lax.rsqrt(jnp.mean(a * a, axis=-1, keepdims=True) + 1e-06)
        x = a * r
        attn[:, hs] = x
        scale[h] = jnp.broadcast_to(r, x.shape)
        normed[:, hs] = (x * gain[:, hs]).astype(bf16)
        return carry

    lax.fori_loop(0, heads, norm_step, 0)

    loads[4].wait()

    def slab(owner):
        return pl.ds(pl.multiple_of(owner * rows, rows), rows)

    def columns(j):
        return pl.ds(pl.multiple_of(j * chunk, chunk), chunk)

    def relay(j, to):
        return pltpu.make_async_remote_copy(
            src_ref=p.at[slab(far), columns(j)],
            dst_ref=rel.at[:, columns(j)],
            send_sem=rel_send.at[j],
            recv_sem=rel_recv.at[j],
            device_id=(c, to),
            device_id_type=MESH,
        )

    def single(h, to, dst):
        cs = pl.ds(h * wing, wing)
        return pltpu.make_async_remote_copy(
            src_ref=p.at[slab(to), cs],
            dst_ref=dst.at[:, cs],
            send_sem=one_send.at[h],
            recv_sem=one_recv.at[h],
            device_id=(c, to),
            device_id_type=MESH,
        )

    def double(j, to, dst):
        return pltpu.make_async_remote_copy(
            src_ref=rel.at[:, columns(j)],
            dst_ref=dst.at[:, columns(j)],
            send_sem=two_send.at[j],
            recv_sem=two_recv.at[j],
            device_id=(c, to),
            device_id_type=MESH,
        )

    n_half = n_chunk // 2

    def project(j):
        cs = columns(j)
        product = nn(normed[...], w[:, cs])
        part[...] = product
        p[:, cs] = product.astype(bf16)
        own[:, cs] = part[slab(y), :]

    def project_step(i, carry):
        project(i)
        relay(i, up).start()
        project(i + n_half)
        relay(i + n_half, down).start()
        return carry

    lax.fori_loop(0, n_half, project_step, 0)
    single(0, down, fin_up).start()
    single(1, up, fin_dn).start()

    wide = 2 * DH

    def cot_columns(h):
        return cot[:, :, h * wing : (h + 1) * wing].reshape(tok, wing)

    def ng_first(i, carry):
        rs = pl.ds(pl.multiple_of(i * wide, wide), wide)
        ng[:, rs] = nt(cot_columns(0), w[rs, :wing])
        return carry

    def ng_second(i, carry):
        rs = pl.ds(pl.multiple_of(i * wide, wide), wide)
        ng[:, rs] += nt(cot_columns(1), w[rs, wing:])
        return carry

    for h in onward_first:
        h.wait_recv()
    lax.fori_loop(0, feat // wide, ng_first, 0)
    for h in onward_second:
        h.wait_recv()
    lax.fori_loop(0, feat // wide, ng_second, 0)

    def norm_back_step(h, carry):
        hs = lanes(h)
        x = attn[:, hs]
        g = ng[:, hs] * gain[:, hs]
        a = scale[h] * (g - x * jnp.mean(g * x, axis=-1, keepdims=True))
        a = a.astype(bf16)
        ag[:, hs] = a
        gs_own[hs, :] = tn(q[:, hs], a).astype(bf16)
        return carry

    lax.fori_loop(0, heads, norm_back_step, 0)
    exchange(gs_own, gs_got, 2)

    def grad_step(h, carry):
        hs = lanes(h)
        a = ag[:, hs]
        masked = jnp.where(causal, nt(a, v[:, hs]), 0.0).astype(bf16)
        dq[:, hs] = (nn(masked, k[:, hs]) + nt(a, st_pre[hs, :])).astype(bf16)
        dk[:, hs] = tn(masked, q[:, hs])
        dv[:, hs] = tn(inner[h], a)
        return carry

    lax.fori_loop(0, heads, grad_step, 0)

    def relay_step(i, carry):
        for j, src, to, dst in ((i, down, up, fin_dn), (i + n_half, up, down, fin_up)):
            cs = columns(j)
            relay(j, to).wait_recv()
            rel[:, cs] = (rel[:, cs].astype(f32) + p[slab(to), cs].astype(f32)).astype(bf16)
            double(j, to, dst).start()
        return carry

    lax.fori_loop(0, n_half - 1, relay_step, 0)

    exchanged(gs_own, gs_got, 2)

    def suffix_step(i, total):
        at = piece_of(n_ctx - 1 - i)
        gs_sum[at, :] = total.astype(bf16)
        return total + gs_got[at, :].astype(f32)

    lax.fori_loop(0, n_ctx, suffix_step, jnp.zeros((share, DH), f32))
    exchange(gs_sum, gs_suf, 3)

    relay_step(n_half - 1, 0)
    exchanged(gs_sum, gs_suf, 3)

    def last_step(h, carry):
        hs = lanes(h)
        dkb[:, hs] = (dk[:, hs] + nt(v[:, hs], gs_suf[hs, :])).astype(bf16)
        dvb[:, hs] = (dv[:, hs] + nn(k[:, hs], gs_suf[hs, :])).astype(bf16)
        return carry

    lax.fori_loop(0, heads, last_step, 0)

    def sum_step(i, carry):
        for j, to, two in ((i, down, fin_dn), (i + n_half, up, fin_up)):
            cs = columns(j)
            double(j, to, two).wait_recv()
            lo[:, cs] = (
                own[:, cs] + (fin_dn[:, cs].astype(f32) + fin_up[:, cs].astype(f32))
            ).astype(bf16)
        return carry

    single(0, down, fin_up).wait_recv()
    single(1, up, fin_dn).wait_recv()
    lax.fori_loop(0, n_half, sum_step, 0)

    for h in (*ups, *downs, *onward_first, *onward_second):
        h.wait_send()

    single(0, down, fin_up).wait_send()
    single(1, up, fin_dn).wait_send()

    def sent_step(j, carry):
        relay(j, up).wait_send()
        double(j, up, fin_dn).wait_send()
        return carry

    lax.fori_loop(0, n_chunk, sent_step, 0)


def store_kernel(*refs):
    sources, results, sem = refs[:4], refs[4:8], refs[8]
    copies = []
    for src, dst in zip(sources, results):
        step = src.shape[0] // N_STORE
        for piece in (pl.ds(i * step, step) for i in range(N_STORE)):
            copies.append(
                pltpu.make_async_copy(src.at[piece], dst.at[piece], sem.at[len(copies)])
            )
    for copy in copies:
        copy.start()
    for copy in copies:
        copy.wait()


def per_device(n_ctx, n_z, n_head, queries, key_rows, value_rows, norm_gain, out_weight, out_cotangent):
    tok, feat = queries.shape
    rows, width = out_cotangent.shape
    heads = feat // DH
    chunk = width // 4
    n_chunk = width // chunk
    state = pltpu.VMEM((feat, DH), bf16)
    any_space = pl.BlockSpec(memory_space=pl.ANY)
    vmem = pl.BlockSpec(memory_space=pltpu.VMEM)
    dma = pltpu.SemaphoreType.DMA
    results = pl.pallas_call(
        functools.partial(kernel, n_ctx, n_z, n_head, chunk),
        out_shape=(
            pltpu.VMEM((rows, width), bf16),
            pltpu.VMEM((tok, feat), bf16),
            pltpu.VMEM((tok, feat), bf16),
            pltpu.VMEM((tok, feat), bf16),
        ),
        in_specs=[any_space, any_space, any_space, vmem, any_space, any_space],
        out_specs=(vmem, vmem, vmem, vmem),
        scratch_shapes=[
            pltpu.VMEM((tok, feat), bf16),
            pltpu.VMEM((tok, feat), bf16),
            pltpu.VMEM((tok, feat), bf16),
            pltpu.VMEM((feat, width), bf16),
            pltpu.VMEM((n_head, rows, width), bf16),
            pltpu.VMEM((heads, tok, tok), bf16),
            pltpu.VMEM((tok, feat), f32),
            pltpu.VMEM((heads, tok, DH), f32),
            pltpu.VMEM((tok, feat), bf16),
            pltpu.VMEM((tok, chunk), f32),
            pltpu.VMEM((rows, width), f32),
            pltpu.VMEM((tok, width), bf16),
            pltpu.VMEM((rows, width), bf16),
            pltpu.VMEM((rows, width), bf16),
            pltpu.VMEM((rows, width), bf16),
            pltpu.VMEM((tok, feat), f32),
            pltpu.VMEM((tok, feat), bf16),
            pltpu.VMEM((tok, feat), f32),
            pltpu.VMEM((tok, feat), f32),
            *[state] * 8,
            dma((5,)),
            pltpu.SemaphoreType.REGULAR,
            pltpu.SemaphoreType.REGULAR,
            dma((8,)),
            dma((8,)),
            dma((4,)),
            dma((4,)),
            *[dma((n_chunk,))] * 6,
        ],
        compiler_params=pltpu.CompilerParams(
            collective_id=0, has_side_effects=True, vmem_limit_bytes=60 * 1024 * 1024
        ),
        cost_estimate=pl.CostEstimate(
            flops=8_000_000_000, bytes_accessed=18_000_000, transcendentals=0
        ),
    )(
        queries,
        key_rows,
        value_rows,
        norm_gain.reshape(1, feat),
        out_weight,
        out_cotangent,
    )
    return pl.pallas_call(
        store_kernel,
        out_shape=tuple(jax.ShapeDtypeStruct(r.shape, r.dtype) for r in results),
        in_specs=[vmem] * 4,
        out_specs=(any_space,) * 4,
        scratch_shapes=[dma((4 * N_STORE,))],
        compiler_params=pltpu.CompilerParams(vmem_limit_bytes=1024 * 1024),
    )(*(pltpu.with_memory_space_constraint(r, pltpu.VMEM) for r in results))


def solution(mesh):
    in_specs = (
        P("ctx", "head"),
        P("ctx", "head"),
        P("ctx", "head"),
        P("head"),
        P("head", None),
        P(("ctx", "head"), None),
    )
    out_specs = (P(("ctx", "head"), None), P("ctx", "head"), P("ctx", "head"), P("ctx", "head"))
    return jax.shard_map(
        functools.partial(per_device, mesh.shape["ctx"], N_Z, mesh.shape["head"]),
        mesh=mesh,
        in_specs=in_specs,
        out_specs=out_specs,
        check_vma=False,
    )
```

```python
import functools

import jax
import jax.numpy as jnp
from jax import lax
from jax.experimental import pallas as pl
from jax.experimental.pallas import tpu as pltpu
from jax.sharding import PartitionSpec as P

DH = 128
N_STORE = 4
N_Z = 4
MESH = pl.DeviceIdType.MESH
f32 = jnp.float32
bf16 = jnp.bfloat16


def nn(a, b):
    return jnp.dot(a, b, preferred_element_type=f32)


def nt(a, b):
    return lax.dot_general(a, b, (((1,), (1,)), ((), ())), preferred_element_type=f32)


def tn(a, b):
    return lax.dot_general(a, b, (((0,), (0,)), ((), ())), preferred_element_type=f32)


def kernel(
    n_ctx,
    n_z,
    n_head,
    chunk,
    q_hbm,
    k_hbm,
    v_hbm,
    gain,
    w_hbm,
    cot_hbm,
    lo,
    dq,
    dkb,
    dvb,
    q,
    k,
    v,
    w,
    cot,
    inner,
    attn,
    scale,
    normed,
    part,
    own,
    p,
    rel,
    fin_dn,
    fin_up,
    ng,
    ag,
    dk,
    dv,
    st_own,
    st_got,
    st_sum,
    st_pre,
    gs_own,
    gs_got,
    gs_sum,
    gs_suf,
    ld_sem,
    ready,
    here,
    ag_send,
    ag_recv,
    sc_send,
    sc_recv,
    rel_send,
    rel_recv,
    one_send,
    one_recv,
    two_send,
    two_recv,
):
    c = lax.axis_index("ctx")
    y = lax.axis_index("head")
    up = lax.rem(y + 1, n_head)
    down = lax.rem(y + n_head - 1, n_head)
    far = lax.rem(y + 2, n_head)
    tok, feat = q.shape
    heads = feat // DH
    rows = cot.shape[1]
    width = cot.shape[2]
    n_chunk = width // chunk
    half = rows // 2
    wing = width // 2
    share = st_own.shape[0] // n_ctx

    loads = [
        pltpu.make_async_copy(src, dst, ld_sem.at[i])
        for i, (src, dst) in enumerate(
            ((k_hbm, k), (v_hbm, v), (q_hbm, q), (cot_hbm, cot.at[y]), (w_hbm, w))
        )
    ]
    barrier = pltpu.get_barrier_semaphore()
    n_group = n_ctx // n_z
    z, g = c // n_group, c % n_group

    def ranked(i):
        x = i // 2
        return 2 * (x + (x // 2) * (1 - 2 * (x % 2))) + i % 2

    rank = ranked(g)

    def signal(sem, to):
        pl.semaphore_signal(sem, inc=1, device_id=(to, y), device_id_type=MESH)

    def greet_member(i, carry):
        signal(barrier, z * n_group + ranked(i))
        return carry

    def greet_line(i, carry):
        signal(barrier, i * n_group + g)
        return carry

    def answer_member(i, carry):
        signal(ready, z * n_group + ranked(i))
        return carry

    def answer_line(i, carry):
        signal(ready, i * n_group + g)
        return carry

    for near in (up, down):
        pl.semaphore_signal(barrier, inc=1, device_id=(c, near), device_id_type=MESH)
    lax.fori_loop(z + 1, n_z, greet_line, 0)
    lax.fori_loop(rank + 1, n_group, greet_member, 0)
    for i in (3, 0, 1, 2, 4):
        loads[i].start()
    loads[3].wait()
    pl.semaphore_wait(barrier, 2 + z + rank)

    def portion(r, h):
        return pl.ds(*r), pl.ds(h * wing, wing)

    every, upper, lower = (0, rows), (0, half), (half, half)

    def hop(src, owner, r, h, to, i):
        return pltpu.make_async_remote_copy(
            src_ref=src.at[portion(r, h)],
            dst_ref=cot.at[(owner, *portion(r, h))],
            send_sem=ag_send.at[i],
            recv_sem=ag_recv.at[i],
            device_id=(c, to),
            device_id_type=MESH,
        )

    ups = [hop(cot.at[y], y, every, h, up, h) for h in (0, 1)]
    downs = [hop(cot.at[y], y, every, h, down, 2 + h) for h in (0, 1)]
    for one, other in zip(ups, downs):
        one.start()
        other.start()
    lax.fori_loop(0, z, answer_line, 0)
    lax.fori_loop(0, rank, answer_member, 0)

    def onward(h):
        ups[h].wait_recv()
        on_up = hop(cot.at[down], down, upper, h, up, 4 + h)
        on_up.start()
        downs[h].wait_recv()
        on_down = hop(cot.at[up], up, lower, h, down, 6 + h)
        on_down.start()
        return on_up, on_down

    def lanes(h):
        return pl.ds(pl.multiple_of(h * DH, DH), DH)

    def piece_of(i):
        return pl.ds(pl.multiple_of(i * share, share), share)

    def exchange(src, dst, i):
        def step(j, carry):
            peer = lax.rem(c + 1 + lax.rem(j + n_ctx // 2, n_ctx - 1), n_ctx)
            pltpu.make_async_remote_copy(
                src_ref=src.at[piece_of(peer)],
                dst_ref=dst.at[piece_of(c)],
                send_sem=sc_send.at[i],
                recv_sem=sc_recv.at[i],
                device_id=(peer, y),
                device_id_type=MESH,
            ).start()
            return carry

        lax.fori_loop(1, n_ctx, step, 0)
        dst[piece_of(c), :] = src[piece_of(c), :]

    def exchanged(src, dst, i):
        whole = pl.ds(0, (n_ctx - 1) * share)
        all_of = pltpu.make_async_remote_copy(
            src_ref=src.at[whole],
            dst_ref=dst.at[whole],
            send_sem=sc_send.at[i],
            recv_sem=sc_recv.at[i],
            device_id=(lax.rem(c + 1, n_ctx), y),
            device_id_type=MESH,
        )
        all_of.wait_send()
        all_of.wait_recv()

    loads[0].wait()
    loads[1].wait()

    def state_step(h, carry):
        hs = lanes(h)
        st_own[hs, :] = tn(k[:, hs], v[:, hs]).astype(bf16)
        return carry

    lax.fori_loop(0, heads, state_step, 0)

    @pl.when(n_z - 1 - z + n_group - 1 - rank > 0)
    def _():
        pl.semaphore_wait(ready, n_z - 1 - z + n_group - 1 - rank)

    def tell_line(i, carry):
        signal(here, lax.rem(z + i, n_z) * n_group + g)
        return carry

    lax.fori_loop(1, n_z, tell_line, 0)
    pl.semaphore_wait(here, n_z - 1)

    exchange(st_own, st_got, 0)

    loads[2].wait()
    causal = lax.broadcasted_iota(jnp.int32, (tok, tok), 0) >= lax.broadcasted_iota(
        jnp.int32, (tok, tok), 1
    )

    def inner_step(h, carry):
        hs = lanes(h)
        masked = jnp.where(causal, nt(q[:, hs], k[:, hs]), 0.0).astype(bf16)
        inner[h] = masked
        attn[:, hs] = nn(masked, v[:, hs])
        return carry

    lax.fori_loop(0, heads, inner_step, 0)

    onward_first = onward(0)
    exchanged(st_own, st_got, 0)

    def prefix_step(i, total):
        st_sum[piece_of(i), :] = total.astype(bf16)
        return total + st_got[piece_of(i), :].astype(f32)

    lax.fori_loop(0, n_ctx, prefix_step, jnp.zeros((share, DH), f32))
    exchange(st_sum, st_pre, 1)
    onward_second = onward(1)
    exchanged(st_sum, st_pre, 1)

    def norm_step(h, carry):
        hs = lanes(h)
        a = attn[:, hs] + nn(q[:, hs], st_pre[hs, :])
        r = lax.rsqrt(jnp.mean(a * a, axis=-1, keepdims=True) + 1e-06)
        x = a * r
        attn[:, hs] = x
        scale[h] = jnp.broadcast_to(r, x.shape)
        normed[:, hs] = (x * gain[:, hs]).astype(bf16)
        return carry

    lax.fori_loop(0, heads, norm_step, 0)

    loads[4].wait()

    def slab(owner):
        return pl.ds(pl.multiple_of(owner * rows, rows), rows)

    def columns(j):
        return pl.ds(pl.multiple_of(j * chunk, chunk), chunk)

    def relay(j, to):
        return pltpu.make_async_remote_copy(
            src_ref=p.at[slab(far), columns(j)],
            dst_ref=rel.at[:, columns(j)],
            send_sem=rel_send.at[j],
            recv_sem=rel_recv.at[j],
            device_id=(c, to),
            device_id_type=MESH,
        )

    def single(h, to, dst):
        cs = pl.ds(h * wing, wing)
        return pltpu.make_async_remote_copy(
            src_ref=p.at[slab(to), cs],
            dst_ref=dst.at[:, cs],
            send_sem=one_send.at[h],
            recv_sem=one_recv.at[h],
            device_id=(c, to),
            device_id_type=MESH,
        )

    def double(j, to, dst):
        return pltpu.make_async_remote_copy(
            src_ref=rel.at[:, columns(j)],
            dst_ref=dst.at[:, columns(j)],
            send_sem=two_send.at[j],
            recv_sem=two_recv.at[j],
            device_id=(c, to),
            device_id_type=MESH,
        )

    n_half = n_chunk // 2

    def project(j):
        cs = columns(j)
        product = nn(normed[...], w[:, cs])
        part[...] = product
        p[:, cs] = product.astype(bf16)
        own[:, cs] = part[slab(y), :]

    def project_step(i, carry):
        project(i)
        relay(i, up).start()
        project(i + n_half)
        relay(i + n_half, down).start()
        return carry

    lax.fori_loop(0, n_half, project_step, 0)
    single(0, down, fin_up).start()
    single(1, up, fin_dn).start()

    wide = 2 * DH

    def cot_columns(h):
        return cot[:, :, h * wing : (h + 1) * wing].reshape(tok, wing)

    def ng_first(i, carry):
        rs = pl.ds(pl.multiple_of(i * wide, wide), wide)
        ng[:, rs] = nt(cot_columns(0), w[rs, :wing])
        return carry

    def ng_second(i, carry):
        rs = pl.ds(pl.multiple_of(i * wide, wide), wide)
        ng[:, rs] += nt(cot_columns(1), w[rs, wing:])
        return carry

    for h in onward_first:
        h.wait_recv()
    lax.fori_loop(0, feat // wide, ng_first, 0)
    for h in onward_second:
        h.wait_recv()
    lax.fori_loop(0, feat // wide, ng_second, 0)

    def norm_back_step(h, carry):
        hs = lanes(h)
        x = attn[:, hs]
        g = ng[:, hs] * gain[:, hs]
        a = scale[h] * (g - x * jnp.mean(g * x, axis=-1, keepdims=True))
        a = a.astype(bf16)
        ag[:, hs] = a
        gs_own[hs, :] = tn(q[:, hs], a).astype(bf16)
        return carry

    lax.fori_loop(0, heads, norm_back_step, 0)
    exchange(gs_own, gs_got, 2)

    def grad_step(h, carry):
        hs = lanes(h)
        a = ag[:, hs]
        masked = jnp.where(causal, nt(a, v[:, hs]), 0.0).astype(bf16)
        dq[:, hs] = (nn(masked, k[:, hs]) + nt(a, st_pre[hs, :])).astype(bf16)
        dk[:, hs] = tn(masked, q[:, hs])
        dv[:, hs] = tn(inner[h], a)
        return carry

    lax.fori_loop(0, heads, grad_step, 0)

    def relay_step(i, carry):
        for j, src, to, dst in ((i, down, up, fin_dn), (i + n_half, up, down, fin_up)):
            cs = columns(j)
            relay(j, to).wait_recv()
            rel[:, cs] = (rel[:, cs].astype(f32) + p[slab(to), cs].astype(f32)).astype(bf16)
            double(j, to, dst).start()
        return carry

    lax.fori_loop(0, n_half - 1, relay_step, 0)

    exchanged(gs_own, gs_got, 2)

    def suffix_step(i, total):
        at = piece_of(n_ctx - 1 - i)
        gs_sum[at, :] = total.astype(bf16)
        return total + gs_got[at, :].astype(f32)

    lax.fori_loop(0, n_ctx, suffix_step, jnp.zeros((share, DH), f32))
    exchange(gs_sum, gs_suf, 3)

    relay_step(n_half - 1, 0)
    exchanged(gs_sum, gs_suf, 3)

    def last_step(h, carry):
        hs = lanes(h)
        dkb[:, hs] = (dk[:, hs] + nt(v[:, hs], gs_suf[hs, :])).astype(bf16)
        dvb[:, hs] = (dv[:, hs] + nn(k[:, hs], gs_suf[hs, :])).astype(bf16)
        return carry

    lax.fori_loop(0, heads, last_step, 0)

    def sum_step(i, carry):
        for j, to, two in ((i, down, fin_dn), (i + n_half, up, fin_up)):
            cs = columns(j)
            double(j, to, two).wait_recv()
            lo[:, cs] = (
                own[:, cs] + (fin_dn[:, cs].astype(f32) + fin_up[:, cs].astype(f32))
            ).astype(bf16)
        return carry

    single(0, down, fin_up).wait_recv()
    single(1, up, fin_dn).wait_recv()
    lax.fori_loop(0, n_half, sum_step, 0)

    for h in (*ups, *downs, *onward_first, *onward_second):
        h.wait_send()

    single(0, down, fin_up).wait_send()
    single(1, up, fin_dn).wait_send()

    def sent_step(j, carry):
        relay(j, up).wait_send()
        double(j, up, fin_dn).wait_send()
        return carry

    lax.fori_loop(0, n_chunk, sent_step, 0)


def store_kernel(*refs):
    sources, results, sem = refs[:4], refs[4:8], refs[8]
    copies = []
    for src, dst in zip(sources, results):
        step = src.shape[0] // N_STORE
        for piece in (pl.ds(i * step, step) for i in range(N_STORE)):
            copies.append(
                pltpu.make_async_copy(src.at[piece], dst.at[piece], sem.at[len(copies)])
            )
    for copy in copies:
        copy.start()
    for copy in copies:
        copy.wait()


def per_device(n_ctx, n_z, n_head, queries, key_rows, value_rows, norm_gain, out_weight, out_cotangent):
    tok, feat = queries.shape
    rows, width = out_cotangent.shape
    heads = feat // DH
    chunk = width // 12
    n_chunk = width // chunk
    state = pltpu.VMEM((feat, DH), bf16)
    any_space = pl.BlockSpec(memory_space=pl.ANY)
    vmem = pl.BlockSpec(memory_space=pltpu.VMEM)
    dma = pltpu.SemaphoreType.DMA
    results = pl.pallas_call(
        functools.partial(kernel, n_ctx, n_z, n_head, chunk),
        out_shape=(
            pltpu.VMEM((rows, width), bf16),
            pltpu.VMEM((tok, feat), bf16),
            pltpu.VMEM((tok, feat), bf16),
            pltpu.VMEM((tok, feat), bf16),
        ),
        in_specs=[any_space, any_space, any_space, vmem, any_space, any_space],
        out_specs=(vmem, vmem, vmem, vmem),
        scratch_shapes=[
            pltpu.VMEM((tok, feat), bf16),
            pltpu.VMEM((tok, feat), bf16),
            pltpu.VMEM((tok, feat), bf16),
            pltpu.VMEM((feat, width), bf16),
            pltpu.VMEM((n_head, rows, width), bf16),
            pltpu.VMEM((heads, tok, tok), bf16),
            pltpu.VMEM((tok, feat), f32),
            pltpu.VMEM((heads, tok, DH), f32),
            pltpu.VMEM((tok, feat), bf16),
            pltpu.VMEM((tok, chunk), f32),
            pltpu.VMEM((rows, width), f32),
            pltpu.VMEM((tok, width), bf16),
            pltpu.VMEM((rows, width), bf16),
            pltpu.VMEM((rows, width), bf16),
            pltpu.VMEM((rows, width), bf16),
            pltpu.VMEM((tok, feat), f32),
            pltpu.VMEM((tok, feat), bf16),
            pltpu.VMEM((tok, feat), f32),
            pltpu.VMEM((tok, feat), f32),
            *[state] * 8,
            dma((5,)),
            pltpu.SemaphoreType.REGULAR,
            pltpu.SemaphoreType.REGULAR,
            dma((8,)),
            dma((8,)),
            dma((4,)),
            dma((4,)),
            *[dma((n_chunk,))] * 6,
        ],
        compiler_params=pltpu.CompilerParams(
            collective_id=0, has_side_effects=True, vmem_limit_bytes=60 * 1024 * 1024
        ),
        cost_estimate=pl.CostEstimate(
            flops=8_000_000_000, bytes_accessed=18_000_000, transcendentals=0
        ),
    )(
        queries,
        key_rows,
        value_rows,
        norm_gain.reshape(1, feat),
        out_weight,
        out_cotangent,
    )
    return pl.pallas_call(
        store_kernel,
        out_shape=tuple(jax.ShapeDtypeStruct(r.shape, r.dtype) for r in results),
        in_specs=[vmem] * 4,
        out_specs=(any_space,) * 4,
        scratch_shapes=[dma((4 * N_STORE,))],
        compiler_params=pltpu.CompilerParams(vmem_limit_bytes=1024 * 1024),
    )(*(pltpu.with_memory_space_constraint(r, pltpu.VMEM) for r in results))


def solution(mesh):
    in_specs = (
        P("ctx", "head"),
        P("ctx", "head"),
        P("ctx", "head"),
        P("head"),
        P("head", None),
        P(("ctx", "head"), None),
    )
    out_specs = (P(("ctx", "head"), None), P("ctx", "head"), P("ctx", "head"), P("ctx", "head"))
    return jax.shard_map(
        functools.partial(per_device, mesh.shape["ctx"], N_Z, mesh.shape["head"]),
        mesh=mesh,
        in_specs=in_specs,
        out_specs=out_specs,
        check_vma=False,
    )
```
